256 devices in a mesh: row: 16 (over x_hi, z), col: 16 (over x_lo, y, core).
Axes of the slice: x: 4 (x_hi: 2, x_lo: 2; x = x_hi * 2 + x_lo), y: 4, z: 8, core: 2. Of those that a mesh axis runs over, the one named last changes fastest.
Arguments:
- pair: float32 [768, 768, 128], P('row', 'col'), may hold values from -6 to 6
- pair_mask: int32 [768, 768], P('row', 'col'), may hold values from 0 to 1, as said below
- ln_gain: float32 [128], replicated, may hold values from 0.25 to 1.75
- ln_bias: float32 [128], replicated, may hold values from -3 to 3
- w_proj: bfloat16 [128, 512], replicated, may hold values from -0.5 to 0.5
- w_gate: bfloat16 [128, 128], replicated, may hold values from -0.5 to 0.5
- out_gain: float32 [128], replicated, may hold values from 0.25 to 1.75
- out_bias: float32 [128], replicated, may hold values from -3 to 3
- w_out: bfloat16 [128, 128], replicated, may hold values from -0.5 to 0.5
Outputs:
- update: float32 [768, 768, 128], P('row', 'col')
The draws below stay inside these ranges and needn't reach their ends.
Inputs may be any that keep to these rules, and one draw needn't show every extreme that they name: pair_mask[i, j] = real[i] * real[j] for a 0/1 flag real of each of the 768 tokens; token 0 is real and token 767 is padding.
All inputs are finite; a program needn't handle non-finite values.
Results may differ from the reference program's by a relative error of at most 0.0033.
Values may be sent and summed in bfloat16 or wider, within the bound.
No kernel may reach another device: no remote copies, remote signals or barrier semaphores. Data moves between devices by JAX's collectives and lax.ppermute only.
A program may use at most 128 MiB of HBM per device.

```python
import jax
import jax.numpy as jnp
from jax import lax

C = 128
HID = 128
N = 768


def draw_pair_mask(key, part):
    key = jax.random.fold_in(key, 5)
    flags = jax.random.randint(key, (N,), 0, 4) > 0
    positions = jnp.arange(N)
    flags = jnp.where(positions == 0, True, flags)
    flags = jnp.where(positions == N - 1, False, flags)
    return (flags[:, None] & flags[None, :]).astype(jnp.int32)


def steps_of(own_key, extent, cuts, least, top_value):
    level, own = 1.0, jax.random.fold_in(own_key, 6)
    for position, shards_of in cuts:
        draws = jnp.exp(jax.random.uniform(jax.random.fold_in(own, position), (shards_of,), jnp.float32, least / len(cuts), top_value / len(cuts)))
        level = level * jnp.repeat(draws, extent[position] // shards_of).reshape([-1 if axis == position else 1 for axis in range(len(extent))])
    return level


def bell_draw(rng, shape, deviation, reach, cuts=(), dtype=jnp.bfloat16):
    values = jax.random.normal(rng, shape, jnp.float32) * deviation
    if len(cuts) > 0:
        values = steps_of(rng, shape, cuts, -0.22, 0.18) * values
    return jnp.clip(values, min=-reach, max=reach).astype(dtype)


def setup_inputs(seed: int = 0) -> dict:
    seeds = jax.random.split(jax.random.key(seed), 10)
    pair = bell_draw(seeds[0], (N, N, C), 1.0, 6.0, ((0, 16), (1, 16)), jnp.float32)
    pair_mask = draw_pair_mask(jax.random.fold_in(seeds[9], 71), 0)
    ln_gain = jnp.clip(1.0 + 0.15 * jax.random.normal(seeds[2], (C,), jnp.float32), 0.25, 1.75)
    ln_bias = bell_draw(seeds[3], (C,), 0.5, 3.0, (), jnp.float32)
    w_proj = bell_draw(seeds[4], (C, 4 * HID), C ** -0.5, 0.5)
    w_gate = bell_draw(seeds[5], (C, C), C ** -0.5, 0.5)
    out_gain = jnp.clip(1.0 + 0.15 * jax.random.normal(seeds[6], (HID,), jnp.float32), 0.25, 1.75)
    out_bias = bell_draw(seeds[7], (HID,), 0.5, 3.0, (), jnp.float32)
    w_out = bell_draw(seeds[8], (HID, C), HID ** -0.5, 0.5)
    return dict(pair=pair, pair_mask=pair_mask, ln_gain=ln_gain, ln_bias=ln_bias, w_proj=w_proj, w_gate=w_gate, out_gain=out_gain, out_bias=out_bias, w_out=w_out)


def layer_norm(values, gain, bias):
    mean = lax.optimization_barrier(jnp.mean(values, axis=-1, keepdims=True))
    centred = values - mean
    var = lax.optimization_barrier(jnp.mean(centred * centred, axis=-1, keepdims=True))
    return centred * lax.rsqrt(var + 1e-05) * gain + bias

def reference(pair, pair_mask, ln_gain, ln_bias, w_proj, w_gate, out_gain, out_bias, w_out):
    tokens, _, chan = pair.shape
    hidden = w_out.shape[0]
    normed = layer_norm(pair, ln_gain, ln_bias).astype(jnp.bfloat16)
    flat = normed.reshape(tokens * tokens, chan)
    proj = jnp.dot(flat, w_proj, preferred_element_type=jnp.float32).reshape(tokens, tokens, 4, hidden)
    keep = pair_mask.astype(jnp.float32)[:, :, None]
    left = (keep * jax.nn.sigmoid(proj[:, :, 0]) * proj[:, :, 1]).astype(jnp.bfloat16)
    right = (keep * jax.nn.sigmoid(proj[:, :, 2]) * proj[:, :, 3]).astype(jnp.bfloat16)
    left_t = jnp.transpose(left, (2, 0, 1)).astype(jnp.float32)
    right_t = jnp.transpose(right, (2, 1, 0)).astype(jnp.float32)
    mixed_t = jnp.matmul(left_t, right_t)
    mixed = jnp.transpose(mixed_t, (1, 2, 0))
    mixed_norm = layer_norm(mixed, out_gain, out_bias).astype(jnp.bfloat16)
    projected = jnp.dot(mixed_norm.reshape(tokens * tokens, hidden), w_out, preferred_element_type=jnp.float32)
    gating = jax.nn.sigmoid(jnp.dot(flat, w_gate, preferred_element_type=jnp.float32))
    return (gating * projected).reshape(tokens, tokens, chan)
```

```python
import jax
import jax.numpy as jnp
from jax import lax
from jax.experimental import pallas as pl
from jax.experimental.pallas import tpu as pltpu
from jax.sharding import Mesh, PartitionSpec as P

EPS = 1e-05
ROW = ("xh", "zh", "zl")
COL = ("xl", "y", "core")
OUT = ("zl", "xl", "y", "xh", "zh")
BACK = ("zl", "xh", "zh", "xl", "y")
F32, BF16 = jnp.float32, jnp.bfloat16


def sigmoid(x):
    return 0.5 * jnp.tanh(0.5 * x) + 0.5


def layer_norm(x, gain, bias, axis):
    mean = jnp.mean(x, axis=axis, keepdims=True)
    centred = x - mean
    var = jnp.mean(centred * centred, axis=axis, keepdims=True)
    return centred * lax.rsqrt(var + EPS) * gain + bias


def project_kernel(pair_ref, mask_ref, gain_ref, bias_ref, w_ref, out_ref, wt_ref):
    @pl.when(pl.program_id(0) == 0)
    def _():
        wt_ref[...] = w_ref[...].astype(F32).T.astype(BF16)

    x = pair_ref[...].reshape(8 * 48, 128)
    normed = layer_norm(x, gain_ref[...], bias_ref[...], -1).astype(BF16)
    normed = normed.reshape(8, 3, 16, 128).transpose(1, 0, 2, 3).reshape(384, 128)
    lane = lax.broadcasted_iota(jnp.int32, (48, 384), 1)
    row = lax.broadcasted_iota(jnp.int32, (48, 384), 0)
    spread = (lane // 128 * 16 + lane % 16 == row).astype(F32)
    keep = jnp.dot(mask_ref[...].astype(F32), spread, preferred_element_type=F32)
    lane8 = lax.broadcasted_iota(jnp.int32, (8, 384), 1)
    row8 = lax.broadcasted_iota(jnp.int32, (8, 384), 0)
    keep = jnp.sum(jnp.where(lane8 // 16 % 8 == row8, keep, 0.0), axis=0, keepdims=True)
    nt = (((1,), (1,)), ((), ()))
    for side in range(2):
        gate = lax.dot_general(wt_ref[side * 256 : side * 256 + 128, :], normed, nt, preferred_element_type=F32)
        value = lax.dot_general(wt_ref[side * 256 + 128 : side * 256 + 256, :], normed, nt, preferred_element_type=F32)
        out_ref[side, 0] = (keep * sigmoid(gate) * value).astype(BF16)


def project(pair, mask, gain, bias, w_proj):
    full = lambda *shape: pl.BlockSpec(shape, lambda i: (0,) * len(shape))
    return pl.pallas_call(
        project_kernel,
        grid=(6,),
        out_shape=jax.ShapeDtypeStruct((2, 2, 128, 1152), BF16),
        in_specs=[
            pl.BlockSpec((8, 48, 128), lambda i: (i, 0, 0)),
            pl.BlockSpec((8, 48), lambda i: (i, 0)),
            full(1, 128),
            full(1, 128),
            full(128, 512),
        ],
        out_specs=pl.BlockSpec((2, 1, 128, 384), lambda i: (0, i // 3, 0, i % 3)),
        scratch_shapes=[pltpu.VMEM((512, 128), BF16)],
        name="project",
    )(pair, mask, gain, bias, w_proj)


def swap_blocks(arrays, block):
    arrays = list(arrays)
    lane = lax.broadcasted_iota(jnp.int32, arrays[0].shape, arrays[0].ndim - 1)
    d = len(arrays) // 2
    while d:
        shift = d * block
        low = (lane & shift) == 0
        for a in range(len(arrays)):
            if a & d == 0:
                p, q = arrays[a], arrays[a + d]
                arrays[a] = jnp.where(low, p, pltpu.roll(q, shift, p.ndim - 1))
                arrays[a + d] = jnp.where(low, pltpu.roll(p, 128 - shift, p.ndim - 1), q)
        d //= 2
    return arrays


def gather_kernel(core_ref, recv_ref, send_ref, keep_ref):
    core = core_ref[0]
    for side in range(2):
        for s in range(18):
            ii_hi, kk_hi = s // 3, s % 3
            tile = recv_ref[side * 2 + s // 9, :, s % 9 * 128 : s % 9 * 128 + 128].astype(F32).reshape(2, 8, 8, 128)
            lanes = slice(kk_hi * 128, kk_hi * 128 + 128)
            for zl in range(2):
                rows = jnp.stack(swap_blocks([tile[zl, c] for c in range(8)], 16))
                tile_rows = rows
                if side == 0:
                    out = tile_rows
                    if zl == 0:
                        first = out
                    else:
                        both = jnp.stack([first, out], axis=1).reshape(128, 128).astype(BF16)
                        send_ref[ii_hi * 128 : ii_hi * 128 + 128, lanes] = both
                else:
                    out = tile_rows.reshape(64, 128).astype(BF16)

                    @pl.when(core == zl)
                    def _():
                        keep_ref[ii_hi * 64 : ii_hi * 64 + 64, lanes] = out

                    @pl.when(core != zl)
                    def _():
                        send_ref[768 + ii_hi * 64 : 768 + ii_hi * 64 + 64, lanes] = out


def gather(core, recv):
    return pl.pallas_call(
        gather_kernel,
        out_shape=(jax.ShapeDtypeStruct((1152, 384), BF16), jax.ShapeDtypeStruct((384, 384), BF16)),
        in_specs=[pl.BlockSpec(memory_space=pltpu.SMEM), pl.BlockSpec(memory_space=pltpu.VMEM)],
        out_specs=(pl.BlockSpec(memory_space=pltpu.VMEM), pl.BlockSpec(memory_space=pltpu.VMEM)),
        name="gather",
    )(core, recv)


def contract_kernel(mine_ref, other_ref, keep_ref, out_ref):
    nt = (((1,), (1,)), ((), ()))
    for i in range(6):
        cols = slice(i * 128, i * 128 + 128)
        mixed = lax.dot_general(keep_ref[...], mine_ref[cols, :], nt, preferred_element_type=F32)
        mixed += lax.dot_general(other_ref[768:, :], other_ref[cols, :], nt, preferred_element_type=F32)
        mixed = mixed.reshape(3, 16, 8, 128)
        for j in range(3):
            s = i * 3 + j
            out = jnp.stack(swap_blocks([mixed[j, a] for a in range(16)], 1))
            out_ref[s // 9, :, s % 9 * 128 : s % 9 * 128 + 128] = out.reshape(128, 128).astype(BF16)


def contract(mine, other, keep):
    return pl.pallas_call(
        contract_kernel,
        out_shape=jax.ShapeDtypeStruct((2, 128, 1152), BF16),
        name="contract",
    )(mine, other, keep)


def gate_kernel(pair_ref, gain_ref, bias_ref, w_ref, out_ref):
    x = pair_ref[...].reshape(8 * 48, 128)
    normed = layer_norm(x, gain_ref[...], bias_ref[...], -1).astype(BF16)
    gate = sigmoid(jnp.dot(normed, w_ref[...], preferred_element_type=F32))
    out_ref[...] = gate.reshape(8, 48, 128)


def gating(pair, gain, bias, w_gate):
    full = lambda *shape: pl.BlockSpec(shape, lambda i: (0,) * len(shape))
    return pl.pallas_call(
        gate_kernel,
        grid=(6,),
        out_shape=jax.ShapeDtypeStruct((48, 48, 128), F32),
        in_specs=[pl.BlockSpec((8, 48, 128), lambda i: (i, 0, 0)), full(1, 128), full(1, 128), full(128, 128)],
        out_specs=pl.BlockSpec((8, 48, 128), lambda i: (i, 0, 0)),
        cost_estimate=pl.CostEstimate(flops=75_000_000, bytes_accessed=2_400_000, transcendentals=300_000),
        name="gate",
    )(pair, gain, bias, w_gate)


def finish_kernel(mixed_ref, gate_ref, gain_ref, bias_ref, w_ref, out_ref):
    mixed = mixed_ref[0].astype(F32)
    normed = layer_norm(mixed, gain_ref[...], bias_ref[...], 0).astype(BF16)
    tn = (((0,), (0,)), ((), ()))
    projected = lax.dot_general(normed, w_ref[...], tn, preferred_element_type=F32)
    projected = projected.reshape(3, 8, 16, 128).transpose(1, 0, 2, 3).reshape(8, 48, 128)
    out_ref[...] = gate_ref[...] * projected


def finish(mixed, gate, gain, bias, w_out):
    full = lambda *shape: pl.BlockSpec(shape, lambda i: (0,) * len(shape))
    return pl.pallas_call(
        finish_kernel,
        grid=(6,),
        out_shape=jax.ShapeDtypeStruct((48, 48, 128), F32),
        in_specs=[
            pl.BlockSpec((1, 128, 384), lambda i: (i // 3, 0, i % 3)),
            pl.BlockSpec((8, 48, 128), lambda i: (i, 0, 0)),
            full(128, 1),
            full(128, 1),
            full(128, 128),
        ],
        out_specs=pl.BlockSpec((8, 48, 128), lambda i: (i, 0, 0)),
        name="finish",
    )(mixed, gate, gain, bias, w_out)


def per_device(pair, pair_mask, ln_gain, ln_bias, w_proj, w_gate, out_gain, out_bias, w_out):
    gain, bias = ln_gain.reshape(1, 128), ln_bias.reshape(1, 128)
    sent = project(pair, pair_mask, gain, bias, w_proj).reshape(4, 128, 1152)
    recv = lax.all_to_all(sent, OUT, 1, 1, tiled=True)
    gate = gating(pair, gain, bias, w_gate)
    core = lax.axis_index("core").astype(jnp.int32).reshape(1)
    mine, keep = gather(core, recv)
    other = lax.ppermute(mine, "core", [(0, 1), (1, 0)])
    mixed = contract(mine, other, keep)
    mixed = lax.all_to_all(mixed, BACK, 1, 1, tiled=True)
    swap = lambda v: v.reshape(2, 8, 8, -1).transpose(0, 2, 1, 3).reshape(128, -1)
    return finish(mixed, gate, swap(out_gain), swap(out_bias), swap(w_out))


def solution(mesh):
    fine = Mesh(mesh.devices.reshape(2, 4, 2, 2, 4, 2), ROW + COL)
    return jax.shard_map(
        per_device,
        mesh=fine,
        in_specs=(P(ROW, COL, None), P(ROW, COL), P(), P(), P(), P(), P(), P(), P()),
        out_specs=P(ROW, COL, None),
        check_vma=False,
    )
```

```python
import jax
import jax.numpy as jnp
from jax import lax
from jax.experimental import pallas as pl
from jax.experimental.pallas import tpu as pltpu
from jax.sharding import Mesh, PartitionSpec as P

EPS = 1e-05
ROW = ("xh", "zh", "zl")
COL = ("xl", "y", "core")
GROUP = ("y", "zh", "zl", "xh", "xl")
F32, BF16 = jnp.float32, jnp.bfloat16
NT = (((1,), (1,)), ((), ()))
TN = (((0,), (0,)), ((), ()))


def sigmoid(x):
    return 0.5 * jnp.tanh(0.5 * x) + 0.5


def layer_norm(x, gain, bias, axis):
    mean = jnp.mean(x, axis=axis, keepdims=True)
    centred = x - mean
    var = jnp.mean(centred * centred, axis=axis, keepdims=True)
    return centred * lax.rsqrt(var + EPS) * gain + bias


def full(*shape):
    return pl.BlockSpec(shape, lambda i: (0,) * len(shape))


def rows_of(place, pair, rows):
    return pl.ds((pair // 2 * 32 + pair % 2) * rows + place, 16, stride=2 * rows)


def project_kernel(pair_ref, mask_ref, gain_ref, bias_ref, w_ref, out_ref, wt_ref, wide_ref):
    step = pl.program_id(0)

    @pl.when(step == 0)
    def _():
        wt_ref[...] = w_ref[...].astype(F32).T.astype(BF16)

    lane = lax.broadcasted_iota(jnp.int32, (48, 384), 1)
    row = lax.broadcasted_iota(jnp.int32, (48, 384), 0)
    spread = (lane // 128 * 16 + lane % 16 == row).astype(F32).astype(BF16)
    keeps = jnp.dot(mask_ref[...].astype(F32).astype(BF16), spread, preferred_element_type=F32)
    lane8 = lax.broadcasted_iota(jnp.int32, (8, 384), 1)
    row8 = lax.broadcasted_iota(jnp.int32, (8, 384), 0)
    for part in range(2):
        x = pair_ref[part * 8 : part * 8 + 8].reshape(8, 3, 16, 128).transpose(1, 0, 2, 3).reshape(384, 128)
        normed = layer_norm(x.T, gain_ref[...], bias_ref[...], 0).astype(BF16)
        keep = jnp.where(lane8 // 16 % 8 == row8, keeps[part * 8 : part * 8 + 8], 0.0)
        keep = jnp.sum(keep, axis=0, keepdims=True)
        for side in range(2):
            gate = jnp.dot(wt_ref[side * 256 : side * 256 + 128, :], normed, preferred_element_type=F32)
            value = jnp.dot(wt_ref[side * 256 + 128 : side * 256 + 256, :], normed, preferred_element_type=F32)
            out = keep * sigmoid(gate) * value
            for kk_hi in range(3):
                at = side * 18 + step * 6 + part * 3 + kk_hi
                wide_ref[pl.ds(at, 128, stride=36), :] = out[:, kk_hi * 128 : kk_hi * 128 + 128]

    @pl.when(step == 2)
    def _():
        out_ref[...] = wide_ref[...].astype(BF16)


def project(pair, mask, gain, bias, w_proj):
    return pl.pallas_call(
        project_kernel,
        grid=(3,),
        out_shape=jax.ShapeDtypeStruct((4608, 128), BF16),
        in_specs=[
            pl.BlockSpec((16, 48, 128), lambda i: (i, 0, 0)),
            pl.BlockSpec((16, 48), lambda i: (i, 0)),
            full(128, 1),
            full(128, 1),
            full(128, 512),
        ],
        out_specs=full(4608, 128),
        scratch_shapes=[pltpu.VMEM((512, 128), BF16), pltpu.VMEM((4608, 128), F32)],
        compiler_params=pltpu.CompilerParams(vmem_limit_bytes=32 << 20),
        name="project",
    )(pair, mask, gain, bias, w_proj)


def gather_kernel(core_ref, recv_ref, swap_ref, send_ref, keep_ref, wide_ref, x_ref, right_ref):
    wide_ref[...] = recv_ref[...].astype(F32)
    for s in range(36):
        for c in range(8):
            x_ref[s * 16 : s * 16 + 16, c * 128 : c * 128 + 128] = wide_ref[rows_of(s, c, 36), :].astype(BF16)
    for n in range(4):
        y = jnp.dot(x_ref[...], swap_ref[:, n * 256 : n * 256 + 256], preferred_element_type=F32).astype(BF16)
        for half in range(2):
            for s in range(36):
                dst = send_ref if s < 18 else right_ref
                at = (s % 18 // 3 * 8 + 2 * n + half) * 16
                lanes = slice(s % 3 * 128, s % 3 * 128 + 128)
                dst[at : at + 16, lanes] = y[s * 16 : s * 16 + 16, half * 128 : half * 128 + 128]
    row = lax.broadcasted_iota(jnp.int32, (128, 256), 0)
    lane = lax.broadcasted_iota(jnp.int32, (128, 256), 1)
    b = row // 16
    for mine in range(2):
        core = core_ref[0] if mine else 1 - core_ref[0]
        pick = (lane // 16 == row % 16) & (lane % 16 == b // 2 * 4 + core * 2 + b % 2)
        pick = pick.astype(F32).astype(BF16)
        for jj_hi in range(3):
            rows = jnp.dot(pick, right_ref[jj_hi * 256 : jj_hi * 256 + 256, :], preferred_element_type=F32).astype(BF16)
            if mine:
                keep_ref[jj_hi * 128 : jj_hi * 128 + 128, :] = rows
            else:
                send_ref[768 + jj_hi * 128 : 768 + jj_hi * 128 + 128, :] = rows


def gather(core, recv, swap):
    vmem = pl.BlockSpec(memory_space=pltpu.VMEM)
    return pl.pallas_call(
        gather_kernel,
        out_shape=(jax.ShapeDtypeStruct((1152, 384), BF16), jax.ShapeDtypeStruct((384, 384), BF16)),
        in_specs=[pl.BlockSpec(memory_space=pltpu.SMEM), vmem, vmem],
        out_specs=(vmem, vmem),
        scratch_shapes=[pltpu.VMEM((4608, 128), F32), pltpu.VMEM((576, 1024), BF16), pltpu.VMEM((768, 384), BF16)],
        compiler_params=pltpu.CompilerParams(vmem_limit_bytes=32 << 20),
        name="gather",
    )(core, recv, swap)


def contract_kernel(mine_ref, other_ref, keep_ref, swap_ref, out_ref, x_ref, wide_ref):
    for i in range(6):
        rows = slice(i * 128, i * 128 + 128)
        mixed = lax.dot_general(mine_ref[rows, :], keep_ref[...], NT, preferred_element_type=F32)
        mixed += lax.dot_general(other_ref[rows, :], other_ref[768:, :], NT, preferred_element_type=F32)
        mixed = mixed.astype(BF16)
        for j in range(3):
            for a in range(8):
                at = (i * 3 + j) * 16
                x_ref[at : at + 16, a * 128 : a * 128 + 128] = mixed[a * 16 : a * 16 + 16, j * 128 : j * 128 + 128]
    for n in range(4):
        y = jnp.dot(x_ref[...], swap_ref[:, n * 256 : n * 256 + 256], preferred_element_type=F32)
        for half in range(2):
            for s in range(18):
                wide_ref[rows_of(s, 2 * n + half, 18), :] = y[s * 16 : s * 16 + 16, half * 128 : half * 128 + 128]
    out_ref[...] = wide_ref[...].astype(BF16)


def contract(mine, other, keep, swap):
    return pl.pallas_call(
        contract_kernel,
        out_shape=jax.ShapeDtypeStruct((2304, 128), BF16),
        scratch_shapes=[pltpu.VMEM((288, 1024), BF16), pltpu.VMEM((2304, 128), F32)],
        compiler_params=pltpu.CompilerParams(vmem_limit_bytes=32 << 20),
        name="contract",
    )(mine, other, keep, swap)


def gate_kernel(pair_ref, gain_ref, bias_ref, w_ref, out_ref):
    x = pair_ref[...].reshape(16 * 48, 128)
    normed = layer_norm(x, gain_ref[...], bias_ref[...], -1).astype(BF16)
    gate = sigmoid(jnp.dot(normed, w_ref[...], preferred_element_type=F32))
    out_ref[...] = gate.reshape(16, 48, 128)


def gating(pair, gain, bias, w_gate):
    return pl.pallas_call(
        gate_kernel,
        grid=(3,),
        out_shape=jax.ShapeDtypeStruct((48, 48, 128), F32),
        in_specs=[pl.BlockSpec((16, 48, 128), lambda i: (i, 0, 0)), full(1, 128), full(1, 128), full(128, 128)],
        out_specs=pl.BlockSpec((16, 48, 128), lambda i: (i, 0, 0)),
        cost_estimate=pl.CostEstimate(flops=75_000_000, bytes_accessed=2_400_000, transcendentals=300_000),
        compiler_params=pltpu.CompilerParams(vmem_limit_bytes=32 << 20),
        name="gate",
    )(pair, gain, bias, w_gate)


def finish_kernel(mixed_ref, gate_ref, gain_ref, bias_ref, w_ref, out_ref, wide_ref):
    step = pl.program_id(0)

    @pl.when(step == 0)
    def _():
        wide_ref[...] = mixed_ref[...].astype(F32)

    for part in range(2):
        at = step * 6 + part * 3
        for jj_hi in range(3):
            mixed = wide_ref[pl.ds(at + jj_hi, 128, stride=18), :]
            normed = layer_norm(mixed, gain_ref[...], bias_ref[...], 0).astype(BF16)
            projected = lax.dot_general(normed, w_ref[...], TN, preferred_element_type=F32).reshape(8, 16, 128)
            rows, cols = slice(part * 8, part * 8 + 8), slice(jj_hi * 16, jj_hi * 16 + 16)
            out_ref[rows, cols, :] = gate_ref[rows, cols, :] * projected


def finish(mixed, gate, gain, bias, w_out):
    return pl.pallas_call(
        finish_kernel,
        grid=(3,),
        out_shape=jax.ShapeDtypeStruct((48, 48, 128), F32),
        in_specs=[
            full(2304, 128),
            pl.BlockSpec((16, 48, 128), lambda i: (i, 0, 0)),
            full(128, 1),
            full(128, 1),
            full(128, 128),
        ],
        out_specs=pl.BlockSpec((16, 48, 128), lambda i: (i, 0, 0)),
        scratch_shapes=[pltpu.VMEM((2304, 128), F32)],
        compiler_params=pltpu.CompilerParams(vmem_limit_bytes=32 << 20),
        name="finish",
    )(mixed, gate, gain, bias, w_out)


def exchange(messages):
    rows = messages.shape[0] // 128
    tiles = messages.reshape(128, 9, rows // 9, 128)
    return lax.all_to_all(tiles, GROUP, 0, 0, tiled=True).reshape(128 * rows, 128)


def per_device(pair, pair_mask, ln_gain, ln_bias, w_proj, w_gate, out_gain, out_bias, w_out):
    recv = exchange(project(pair, pair_mask, ln_gain.reshape(128, 1), ln_bias.reshape(128, 1), w_proj))
    gate = gating(pair, ln_gain.reshape(1, 128), ln_bias.reshape(1, 128), w_gate)
    place = jnp.arange(1024)
    target = place // 16 % 8 * 128 + place // 128 * 16 + place % 16
    swap = (target[:, None] == place[None, :]).astype(BF16)
    core = lax.axis_index("core").astype(jnp.int32).reshape(1)
    mine, keep = gather(core, recv, swap)
    other = lax.ppermute(mine, "core", [(0, 1), (1, 0)])
    mixed = exchange(contract(mine, other, keep, swap))
    return finish(mixed, gate, out_gain.reshape(128, 1), out_bias.reshape(128, 1), w_out)


def solution(mesh):
    fine = Mesh(mesh.devices.reshape(2, 4, 2, 2, 4, 2), ROW + COL)
    return jax.shard_map(
        per_device,
        mesh=fine,
        in_specs=(P(ROW, COL, None), P(ROW, COL), P(), P(), P(), P(), P(), P(), P()),
        out_specs=P(ROW, COL, None),
        check_vma=False,
    )
```

```python
import jax
import jax.numpy as jnp
from jax import lax
from jax.experimental import pallas as pl
from jax.experimental.pallas import tpu as pltpu
from jax.sharding import Mesh, PartitionSpec as P

EPS = 1e-05
ROW = ("xh", "zh", "zl")
COL = ("xl", "y", "core")
GROUP = ("y", "zh", "zl", "xh", "xl")
F32, BF16 = jnp.float32, jnp.bfloat16
NT = (((1,), (1,)), ((), ()))
TN = (((0,), (0,)), ((), ()))


def sigmoid(x):
    return 0.5 * jnp.tanh(0.5 * x) + 0.5


def layer_norm(x, gain, bias, axis):
    mean = jnp.mean(x, axis=axis, keepdims=True)
    centred = x - mean
    var = jnp.mean(centred * centred, axis=axis, keepdims=True)
    return centred * lax.rsqrt(var + EPS) * gain + bias


def column(row):
    return jnp.broadcast_to(row, (8, 128)).T[:, :1]


def full(*shape):
    return pl.BlockSpec(shape, lambda i: (0,) * len(shape))


def rows_of(place, pair, rows):
    return pl.ds((pair // 2 * 32 + pair % 2) * rows + place, 16, stride=2 * rows)


def project_kernel(pair_ref, mask_ref, gain_ref, bias_ref, w_ref, out_ref, wt_ref, wide_ref):
    step = pl.program_id(0)

    @pl.when(step == 0)
    def _():
        wt_ref[...] = w_ref[...].astype(F32).T.astype(BF16)

    lane = lax.broadcasted_iota(jnp.int32, (48, 384), 1)
    row = lax.broadcasted_iota(jnp.int32, (48, 384), 0)
    spread = (lane // 128 * 16 + lane % 16 == row).astype(F32).astype(BF16)
    keeps = jnp.dot(mask_ref[...].astype(F32).astype(BF16), spread, preferred_element_type=F32)
    lane8 = lax.broadcasted_iota(jnp.int32, (8, 384), 1)
    row8 = lax.broadcasted_iota(jnp.int32, (8, 384), 0)
    gain, bias = column(gain_ref[...]), column(bias_ref[...])
    for part in range(2):
        x = pair_ref[part * 8 : part * 8 + 8].reshape(8, 3, 16, 128).transpose(1, 0, 2, 3).reshape(384, 128)
        normed = layer_norm(x.T, gain, bias, 0).astype(BF16)
        keep = jnp.where(lane8 // 16 % 8 == row8, keeps[part * 8 : part * 8 + 8], 0.0)
        keep = jnp.sum(keep, axis=0, keepdims=True)
        for side in range(2):
            gate = jnp.dot(wt_ref[side * 256 : side * 256 + 128, :], normed, preferred_element_type=F32)
            value = jnp.dot(wt_ref[side * 256 + 128 : side * 256 + 256, :], normed, preferred_element_type=F32)
            out = keep * sigmoid(gate) * value
            for kk_hi in range(3):
                at = side * 18 + step * 6 + part * 3 + kk_hi
                wide_ref[pl.ds(at, 128, stride=36), :] = out[:, kk_hi * 128 : kk_hi * 128 + 128]

    @pl.when(step == 2)
    def _():
        out_ref[...] = wide_ref[...].astype(BF16)


def project(pair, mask, gain, bias, w_proj):
    return pl.pallas_call(
        project_kernel,
        grid=(3,),
        out_shape=jax.ShapeDtypeStruct((4608, 128), BF16),
        in_specs=[
            pl.BlockSpec((16, 48, 128), lambda i: (i, 0, 0)),
            pl.BlockSpec((16, 48), lambda i: (i, 0)),
            full(1, 128),
            full(1, 128),
            full(128, 512),
        ],
        out_specs=full(4608, 128),
        scratch_shapes=[pltpu.VMEM((512, 128), BF16), pltpu.VMEM((4608, 128), F32)],
        compiler_params=pltpu.CompilerParams(vmem_limit_bytes=60 << 20),
        name="project",
    )(pair, mask, gain, bias, w_proj)


def gather_kernel(core_ref, recv_ref, swap_ref, send_ref, keep_ref, wide_ref, x_ref, right_ref):
    wide_ref[...] = recv_ref[...].astype(F32)
    for s in range(36):
        for c in range(8):
            x_ref[s * 16 : s * 16 + 16, c * 128 : c * 128 + 128] = wide_ref[rows_of(s, c, 36), :].astype(BF16)
    for n in range(4):
        y = jnp.dot(x_ref[...], swap_ref[:, n * 256 : n * 256 + 256], preferred_element_type=F32).astype(BF16)
        for half in range(2):
            for s in range(36):
                dst = send_ref if s < 18 else right_ref
                at = (s % 18 // 3 * 8 + 2 * n + half) * 16
                lanes = slice(s % 3 * 128, s % 3 * 128 + 128)
                dst[at : at + 16, lanes] = y[s * 16 : s * 16 + 16, half * 128 : half * 128 + 128]
    row = lax.broadcasted_iota(jnp.int32, (128, 256), 0)
    lane = lax.broadcasted_iota(jnp.int32, (128, 256), 1)
    b = row // 16
    for mine in range(2):
        core = core_ref[0] if mine else 1 - core_ref[0]
        pick = (lane // 16 == row % 16) & (lane % 16 == b // 2 * 4 + core * 2 + b % 2)
        pick = pick.astype(F32).astype(BF16)
        for jj_hi in range(3):
            rows = jnp.dot(pick, right_ref[jj_hi * 256 : jj_hi * 256 + 256, :], preferred_element_type=F32).astype(BF16)
            if mine:
                keep_ref[jj_hi * 128 : jj_hi * 128 + 128, :] = rows
            else:
                send_ref[768 + jj_hi * 128 : 768 + jj_hi * 128 + 128, :] = rows


def gather(core, recv, swap):
    vmem = pl.BlockSpec(memory_space=pltpu.VMEM)
    return pl.pallas_call(
        gather_kernel,
        out_shape=(jax.ShapeDtypeStruct((1152, 384), BF16), jax.ShapeDtypeStruct((384, 384), BF16)),
        in_specs=[pl.BlockSpec(memory_space=pltpu.SMEM), vmem, vmem],
        out_specs=(vmem, vmem),
        scratch_shapes=[pltpu.VMEM((4608, 128), F32), pltpu.VMEM((576, 1024), BF16), pltpu.VMEM((768, 384), BF16)],
        compiler_params=pltpu.CompilerParams(vmem_limit_bytes=32 << 20),
        name="gather",
    )(core, recv, swap)


def contract_kernel(mine_ref, other_ref, keep_ref, swap_ref, out_ref, x_ref, wide_ref):
    for i in range(6):
        rows = slice(i * 128, i * 128 + 128)
        mixed = lax.dot_general(mine_ref[rows, :], keep_ref[...], NT, preferred_element_type=F32)
        mixed += lax.dot_general(other_ref[rows, :], other_ref[768:, :], NT, preferred_element_type=F32)
        mixed = mixed.astype(BF16)
        for j in range(3):
            for a in range(8):
                at = (i * 3 + j) * 16
                x_ref[at : at + 16, a * 128 : a * 128 + 128] = mixed[a * 16 : a * 16 + 16, j * 128 : j * 128 + 128]
    for n in range(4):
        y = jnp.dot(x_ref[...], swap_ref[:, n * 256 : n * 256 + 256], preferred_element_type=F32)
        for half in range(2):
            for s in range(18):
                wide_ref[rows_of(s, 2 * n + half, 18), :] = y[s * 16 : s * 16 + 16, half * 128 : half * 128 + 128]
    out_ref[...] = wide_ref[...].astype(BF16)


def contract(mine, other, keep, swap):
    return pl.pallas_call(
        contract_kernel,
        out_shape=jax.ShapeDtypeStruct((2304, 128), BF16),
        scratch_shapes=[pltpu.VMEM((288, 1024), BF16), pltpu.VMEM((2304, 128), F32)],
        compiler_params=pltpu.CompilerParams(vmem_limit_bytes=32 << 20),
        name="contract",
    )(mine, other, keep, swap)


def gate_kernel(pair_ref, gain_ref, bias_ref, w_ref, out_ref):
    x = pair_ref[...].reshape(16 * 48, 128)
    normed = layer_norm(x, gain_ref[...], bias_ref[...], -1).astype(BF16)
    gate = sigmoid(jnp.dot(normed, w_ref[...], preferred_element_type=F32))
    out_ref[...] = gate.reshape(16, 48, 128)


def gating(pair, gain, bias, w_gate):
    return pl.pallas_call(
        gate_kernel,
        grid=(3,),
        out_shape=jax.ShapeDtypeStruct((48, 48, 128), F32),
        in_specs=[pl.BlockSpec((16, 48, 128), lambda i: (i, 0, 0)), full(1, 128), full(1, 128), full(128, 128)],
        out_specs=pl.BlockSpec((16, 48, 128), lambda i: (i, 0, 0)),
        cost_estimate=pl.CostEstimate(flops=75_000_000, bytes_accessed=2_400_000, transcendentals=300_000),
        compiler_params=pltpu.CompilerParams(vmem_limit_bytes=32 << 20),
        name="gate",
    )(pair, gain, bias, w_gate)


def finish_kernel(mixed_ref, gate_ref, gain_ref, bias_ref, w_ref, out_ref, wide_ref):
    step = pl.program_id(0)

    @pl.when(step == 0)
    def _():
        wide_ref[...] = mixed_ref[...].astype(F32)

    gain, bias = column(gain_ref[...]), column(bias_ref[...])
    for part in range(2):
        at = step * 6 + part * 3
        for jj_hi in range(3):
            mixed = wide_ref[pl.ds(at + jj_hi, 128, stride=18), :]
            normed = layer_norm(mixed, gain, bias, 0).astype(BF16)
            projected = lax.dot_general(normed, w_ref[...], TN, preferred_element_type=F32).reshape(8, 16, 128)
            rows, cols = slice(part * 8, part * 8 + 8), slice(jj_hi * 16, jj_hi * 16 + 16)
            out_ref[rows, cols, :] = gate_ref[rows, cols, :] * projected


def finish(mixed, gate, gain, bias, w_out):
    return pl.pallas_call(
        finish_kernel,
        grid=(3,),
        out_shape=jax.ShapeDtypeStruct((48, 48, 128), F32),
        in_specs=[
            full(2304, 128),
            pl.BlockSpec((16, 48, 128), lambda i: (i, 0, 0)),
            full(1, 128),
            full(1, 128),
            full(128, 128),
        ],
        out_specs=pl.BlockSpec((16, 48, 128), lambda i: (i, 0, 0)),
        scratch_shapes=[pltpu.VMEM((2304, 128), F32)],
        compiler_params=pltpu.CompilerParams(vmem_limit_bytes=32 << 20),
        name="finish",
    )(mixed, gate, gain, bias, w_out)


def exchange(messages):
    rows = messages.shape[0] // 128
    tiles = messages.reshape(128, 9, rows // 9, 128)
    return lax.all_to_all(tiles, GROUP, 0, 0, tiled=True).reshape(128 * rows, 128)


def per_device(pair, pair_mask, ln_gain, ln_bias, w_proj, w_gate, out_gain, out_bias, w_out):
    recv = exchange(project(pair, pair_mask, ln_gain.reshape(1, 128), ln_bias.reshape(1, 128), w_proj))
    gate = gating(pair, ln_gain.reshape(1, 128), ln_bias.reshape(1, 128), w_gate)
    place = jnp.arange(1024)
    target = place // 16 % 8 * 128 + place // 128 * 16 + place % 16
    swap = (target[:, None] == place[None, :]).astype(BF16)
    core = lax.axis_index("core").astype(jnp.int32).reshape(1)
    mine, keep = gather(core, recv, swap)
    other = lax.ppermute(mine, "core", [(0, 1), (1, 0)])
    mixed = exchange(contract(mine, other, keep, swap))
    return finish(mixed, gate, out_gain.reshape(1, 128), out_bias.reshape(1, 128), w_out)


def solution(mesh):
    fine = Mesh(mesh.devices.reshape(2, 4, 2, 2, 4, 2), ROW + COL)
    return jax.shard_map(
        per_device,
        mesh=fine,
        in_specs=(P(ROW, COL, None), P(ROW, COL), P(), P(), P(), P(), P(), P(), P()),
        out_specs=P(ROW, COL, None),
        check_vma=False,
    )
```

```python
import jax
import jax.numpy as jnp
import numpy as np
from jax import lax
from jax.experimental import pallas as pl
from jax.experimental.pallas import tpu as pltpu
from jax.sharding import Mesh, PartitionSpec as P

EPS = 1e-05
ROW = ("xh", "zh", "zl")
COL = ("xl", "y", "core")
GROUP = ("y", "zh", "zl", "xh", "xl")
F32, BF16 = jnp.float32, jnp.bfloat16
NT = (((1,), (1,)), ((), ()))
TN = (((0,), (0,)), ((), ()))


def sigmoid(x):
    return 0.5 * jnp.tanh(0.5 * x) + 0.5


def layer_norm(x, gain, bias, axis):
    mean = jnp.mean(x, axis=axis, keepdims=True)
    centred = x - mean
    var = jnp.mean(centred * centred, axis=axis, keepdims=True)
    return centred * lax.rsqrt(var + EPS) * gain + bias


def column(row):
    return jnp.broadcast_to(row, (8, 128)).T[:, :1]


def full(*shape):
    return pl.BlockSpec(shape, lambda i: (0,) * len(shape))


def rows_of(place, pair, rows):
    return pl.ds((pair // 2 * 32 + pair % 2) * rows + place, 16, stride=2 * rows)


def project_kernel(
    pair_hbm, mask_hbm, gain_hbm, bias_hbm, w_hbm, out_ref,
    pair_ref, mask_ref, gain_ref, bias_ref, w_ref, wt_ref, wide_ref, sems,
):
    small = [
        pltpu.make_async_copy(src, dst, sems.at[6 + n])
        for n, (src, dst) in enumerate(((w_hbm, w_ref), (gain_hbm, gain_ref), (bias_hbm, bias_ref), (mask_hbm, mask_ref)))
    ]
    chunks = [
        pltpu.make_async_copy(pair_hbm.at[pl.ds(part * 8, 8)], pair_ref.at[pl.ds(part * 8, 8)], sems.at[part])
        for part in range(6)
    ]
    small[0].start()
    chunks[0].start()
    for copy in small[1:] + chunks[1:]:
        copy.start()
    lane = lax.broadcasted_iota(jnp.int32, (48, 384), 1)
    row = lax.broadcasted_iota(jnp.int32, (48, 384), 0)
    spread = (lane // 128 * 16 + lane % 16 == row).astype(F32).astype(BF16)
    own = lax.broadcasted_iota(jnp.int32, (8, 384), 1) // 16 % 8 == lax.broadcasted_iota(jnp.int32, (8, 384), 0)
    for copy in small + chunks:
        copy.wait()
    wt_ref[...] = w_ref[...].astype(F32).T.astype(BF16)
    keeps = jnp.dot(mask_ref[...].astype(F32).astype(BF16), spread, preferred_element_type=F32)
    gain, bias = column(gain_ref[...]), column(bias_ref[...])
    for part in range(6):
        x = pair_ref[part * 8 : part * 8 + 8].reshape(8, 3, 16, 128).transpose(1, 0, 2, 3).reshape(384, 128)
        normed = layer_norm(x.T, gain, bias, 0).astype(BF16)
        keep = jnp.sum(jnp.where(own, keeps[part * 8 : part * 8 + 8], 0.0), axis=0, keepdims=True)
        for side in range(2):
            gate = jnp.dot(wt_ref[side * 256 : side * 256 + 128, :], normed, preferred_element_type=F32)
            value = jnp.dot(wt_ref[side * 256 + 128 : side * 256 + 256, :], normed, preferred_element_type=F32)
            out = keep * sigmoid(gate) * value
            for kk_hi in range(3):
                at = side * 18 + part * 3 + kk_hi
                wide_ref[pl.ds(at, 128, stride=36), :] = out[:, kk_hi * 128 : kk_hi * 128 + 128]
    out_ref[...] = wide_ref[...].astype(BF16)


def project(pair, mask, gain, bias, w_proj):
    return pl.pallas_call(
        project_kernel,
        out_shape=pltpu.VMEM((4608, 128), BF16),
        in_specs=[pl.BlockSpec(memory_space=pltpu.HBM)] * 5,
        out_specs=pl.BlockSpec(memory_space=pltpu.VMEM),
        scratch_shapes=[
            pltpu.VMEM((48, 48, 128), F32),
            pltpu.VMEM((48, 48), jnp.int32),
            pltpu.VMEM((1, 128), F32),
            pltpu.VMEM((1, 128), F32),
            pltpu.VMEM((128, 512), BF16),
            pltpu.VMEM((512, 128), BF16),
            pltpu.VMEM((4608, 128), F32),
            pltpu.SemaphoreType.DMA((10,)),
        ],
        compiler_params=pltpu.CompilerParams(vmem_limit_bytes=32 << 20),
        name="project",
    )(*(pltpu.with_memory_space_constraint(x, pltpu.HBM) for x in (pair, mask, gain, bias, w_proj)))


def gather_kernel(core_ref, recv_ref, swap_ref, send_ref, keep_ref, wide_ref, x_ref, right_ref):
    wide_ref[...] = recv_ref[...].astype(F32)
    for s in range(36):
        for c in range(8):
            x_ref[s * 16 : s * 16 + 16, c * 128 : c * 128 + 128] = wide_ref[rows_of(s, c, 36), :].astype(BF16)
    for n in range(4):
        y = jnp.dot(x_ref[...], swap_ref[:, n * 256 : n * 256 + 256], preferred_element_type=F32).astype(BF16)
        for half in range(2):
            for s in range(36):
                dst = send_ref if s < 18 else right_ref
                at = (s % 18 // 3 * 8 + 2 * n + half) * 16
                lanes = slice(s % 3 * 128, s % 3 * 128 + 128)
                dst[at : at + 16, lanes] = y[s * 16 : s * 16 + 16, half * 128 : half * 128 + 128]
    row = lax.broadcasted_iota(jnp.int32, (128, 256), 0)
    lane = lax.broadcasted_iota(jnp.int32, (128, 256), 1)
    b = row // 16
    for mine in range(2):
        core = core_ref[0] if mine else 1 - core_ref[0]
        pick = (lane // 16 == row % 16) & (lane % 16 == b // 2 * 4 + core * 2 + b % 2)
        pick = pick.astype(F32).astype(BF16)
        for jj_hi in range(3):
            rows = jnp.dot(pick, right_ref[jj_hi * 256 : jj_hi * 256 + 256, :], preferred_element_type=F32).astype(BF16)
            if mine:
                keep_ref[jj_hi * 128 : jj_hi * 128 + 128, :] = rows
            else:
                send_ref[768 + jj_hi * 128 : 768 + jj_hi * 128 + 128, :] = rows


def gather(core, recv, swap):
    vmem = pl.BlockSpec(memory_space=pltpu.VMEM)
    return pl.pallas_call(
        gather_kernel,
        out_shape=(jax.ShapeDtypeStruct((1152, 384), BF16), jax.ShapeDtypeStruct((384, 384), BF16)),
        in_specs=[pl.BlockSpec(memory_space=pltpu.SMEM), vmem, vmem],
        out_specs=(vmem, vmem),
        scratch_shapes=[pltpu.VMEM((4608, 128), F32), pltpu.VMEM((576, 1024), BF16), pltpu.VMEM((768, 384), BF16)],
        compiler_params=pltpu.CompilerParams(vmem_limit_bytes=32 << 20),
        name="gather",
    )(core, recv, swap)


def contract_kernel(mine_ref, other_ref, keep_ref, swap_ref, out_ref, x_ref, wide_ref):
    for i in range(6):
        rows = slice(i * 128, i * 128 + 128)
        mixed = lax.dot_general(mine_ref[rows, :], keep_ref[...], NT, preferred_element_type=F32)
        mixed += lax.dot_general(other_ref[rows, :], other_ref[768:, :], NT, preferred_element_type=F32)
        mixed = mixed.astype(BF16)
        for j in range(3):
            for a in range(8):
                at = (i * 3 + j) * 16
                x_ref[at : at + 16, a * 128 : a * 128 + 128] = mixed[a * 16 : a * 16 + 16, j * 128 : j * 128 + 128]
    for n in range(4):
        y = jnp.dot(x_ref[...], swap_ref[:, n * 256 : n * 256 + 256], preferred_element_type=F32)
        for half in range(2):
            for s in range(18):
                wide_ref[rows_of(s, 2 * n + half, 18), :] = y[s * 16 : s * 16 + 16, half * 128 : half * 128 + 128]
    out_ref[...] = wide_ref[...].astype(BF16)


def contract(mine, other, keep, swap):
    return pl.pallas_call(
        contract_kernel,
        out_shape=jax.ShapeDtypeStruct((2304, 128), BF16),
        scratch_shapes=[pltpu.VMEM((288, 1024), BF16), pltpu.VMEM((2304, 128), F32)],
        compiler_params=pltpu.CompilerParams(vmem_limit_bytes=32 << 20),
        name="contract",
    )(mine, other, keep, swap)


def gate_kernel(pair_ref, gain_ref, bias_ref, w_ref, out_ref):
    x = pair_ref[...].reshape(16 * 48, 128)
    normed = layer_norm(x, gain_ref[...], bias_ref[...], -1).astype(BF16)
    gate = sigmoid(jnp.dot(normed, w_ref[...], preferred_element_type=F32))
    out_ref[...] = gate.reshape(16, 48, 128)


def gating(pair, gain, bias, w_gate):
    return pl.pallas_call(
        gate_kernel,
        grid=(3,),
        out_shape=jax.ShapeDtypeStruct((48, 48, 128), F32),
        in_specs=[pl.BlockSpec((16, 48, 128), lambda i: (i, 0, 0)), full(1, 128), full(1, 128), full(128, 128)],
        out_specs=pl.BlockSpec((16, 48, 128), lambda i: (i, 0, 0)),
        cost_estimate=pl.CostEstimate(flops=75_000_000, bytes_accessed=2_400_000, transcendentals=300_000),
        compiler_params=pltpu.CompilerParams(vmem_limit_bytes=32 << 20),
        name="gate",
    )(pair, gain, bias, w_gate)


def finish_kernel(mixed_ref, gate_ref, gain_ref, bias_ref, w_ref, out_hbm, wide_ref, out_ref, sems):
    wide_ref[...] = mixed_ref[...].astype(F32)
    gain, bias = column(gain_ref[...]), column(bias_ref[...])
    copies = []
    for part in range(6):
        for jj_hi in range(3):
            mixed = wide_ref[pl.ds(part * 3 + jj_hi, 128, stride=18), :]
            normed = layer_norm(mixed, gain, bias, 0).astype(BF16)
            projected = lax.dot_general(normed, w_ref[...], TN, preferred_element_type=F32).reshape(8, 16, 128)
            rows, cols = slice(part * 8, part * 8 + 8), slice(jj_hi * 16, jj_hi * 16 + 16)
            out_ref[rows, cols, :] = gate_ref[rows, cols, :] * projected
        rows = pl.ds(part * 8, 8)
        copies.append(pltpu.make_async_copy(out_ref.at[rows], out_hbm.at[rows], sems.at[part]))
        copies[-1].start()
    for copy in copies:
        copy.wait()


def finish(mixed, gate, gain, bias, w_out):
    return pl.pallas_call(
        finish_kernel,
        out_shape=jax.ShapeDtypeStruct((48, 48, 128), F32),
        in_specs=[pl.BlockSpec(memory_space=pltpu.VMEM)] * 5,
        out_specs=pl.BlockSpec(memory_space=pltpu.HBM),
        scratch_shapes=[pltpu.VMEM((2304, 128), F32), pltpu.VMEM((48, 48, 128), F32), pltpu.SemaphoreType.DMA((6,))],
        compiler_params=pltpu.CompilerParams(vmem_limit_bytes=32 << 20),
        name="finish",
    )(mixed, gate, gain, bias, w_out)


def exchange(messages):
    rows = messages.shape[0] // 128
    tiles = messages.reshape(128, 9, rows // 9, 128)
    return lax.all_to_all(tiles, GROUP, 0, 0, tiled=True).reshape(128 * rows, 128)


def per_device(pair, pair_mask, ln_gain, ln_bias, w_proj, w_gate, out_gain, out_bias, w_out):
    hold = lax.optimization_barrier
    gain, bias = ln_gain.reshape(1, 128), ln_bias.reshape(1, 128)
    sent = project(pair, pair_mask, gain, bias, w_proj)
    core = lax.axis_index("core").astype(jnp.int32).reshape(1)
    sent, core = hold((sent, core))
    recv, pair, gain, bias, w_gate, w_out, out_gain, out_bias = hold(
        (exchange(sent), pair, gain, bias, w_gate, w_out, out_gain, out_bias)
    )
    place = np.arange(1024)
    swap = jnp.asarray(place[None, :] == (place // 16 % 8 * 128 + place // 128 * 16 + place % 16)[:, None], BF16)
    mine, keep = gather(core, recv, swap)
    other = lax.ppermute(mine, "core", [(0, 1), (1, 0)])
    gate = gating(pair, gain, bias, w_gate)
    sent, gate, w_out, out_gain, out_bias = hold((contract(mine, other, keep, swap), gate, w_out, out_gain, out_bias))
    mixed, gate, w_out, out_gain, out_bias = hold((exchange(sent), gate, w_out, out_gain, out_bias))
    return finish(mixed, gate, out_gain.reshape(1, 128), out_bias.reshape(1, 128), w_out)


def solution(mesh):
    fine = Mesh(mesh.devices.reshape(2, 4, 2, 2, 4, 2), ROW + COL)
    return jax.shard_map(
        per_device,
        mesh=fine,
        in_specs=(P(ROW, COL, None), P(ROW, COL), P(), P(), P(), P(), P(), P(), P()),
        out_specs=P(ROW, COL, None),
        check_vma=False,
    )
```

```python
import jax
import jax.numpy as jnp
import numpy as np
from jax import lax
from jax.experimental import pallas as pl
from jax.experimental.pallas import tpu as pltpu
from jax.sharding import Mesh, PartitionSpec as P

EPS = 1e-05
ROW = ("xh", "zh", "zl")
COL = ("xl", "y", "core")
GROUP = ("y", "zh", "zl", "xh", "xl")
F32, BF16 = jnp.float32, jnp.bfloat16
NT = (((1,), (1,)), ((), ()))
TN = (((0,), (0,)), ((), ()))


def sigmoid(x):
    return 0.5 * jnp.tanh(0.5 * x) + 0.5


def layer_norm(x, gain, bias, axis):
    mean = jnp.mean(x, axis=axis, keepdims=True)
    centred = x - mean
    var = jnp.mean(centred * centred, axis=axis, keepdims=True)
    return centred * lax.rsqrt(var + EPS) * gain + bias


def column(row):
    return jnp.broadcast_to(row, (8, 128)).T[:, :1]


def full(*shape):
    return pl.BlockSpec(shape, lambda i: (0,) * len(shape))


def rows_of(place, pair, rows):
    return pl.ds((pair // 2 * 32 + pair % 2) * rows + place, 16, stride=2 * rows)


def project_kernel(
    pair_hbm, mask_hbm, gain_hbm, bias_hbm, w_hbm, w_gate_hbm, out_ref, gate_ref,
    pair_ref, mask_ref, gain_ref, bias_ref, w_ref, w_gate_ref, wt_ref, normed_ref, wide_ref, sems,
):
    small = [
        pltpu.make_async_copy(src, dst, sems.at[6 + n])
        for n, (src, dst) in enumerate(
            (
                (w_hbm, w_ref),
                (gain_hbm, gain_ref),
                (bias_hbm, bias_ref),
                (mask_hbm, mask_ref),
                (w_gate_hbm, w_gate_ref),
            )
        )
    ]
    chunks = [
        pltpu.make_async_copy(pair_hbm.at[pl.ds(part * 8, 8)], pair_ref.at[pl.ds(part * 8, 8)], sems.at[part])
        for part in range(6)
    ]
    for copy in chunks[:2] + small + chunks[2:]:
        copy.start()
    lane = lax.broadcasted_iota(jnp.int32, (48, 384), 1)
    row = lax.broadcasted_iota(jnp.int32, (48, 384), 0)
    spread = (lane // 128 * 16 + lane % 16 == row).astype(F32).astype(BF16)
    own = lax.broadcasted_iota(jnp.int32, (8, 384), 1) // 16 % 8 == lax.broadcasted_iota(jnp.int32, (8, 384), 0)
    for copy in small + chunks[:2]:
        copy.wait()
    wt_ref[...] = w_ref[...].astype(F32).T.astype(BF16)
    keeps = jnp.dot(mask_ref[...].astype(F32).astype(BF16), spread, preferred_element_type=F32)
    gain, bias = column(gain_ref[...]), column(bias_ref[...])

    def norm(part):
        x = pair_ref[part * 8 : part * 8 + 8].reshape(8, 3, 16, 128).transpose(1, 0, 2, 3).reshape(384, 128)
        return layer_norm(x.T, gain, bias, 0).astype(BF16)

    for part in range(2):
        normed_ref[part] = norm(part)
    for copy in chunks[2:]:
        copy.wait()
    for part in range(6):
        normed = normed_ref[part] if part < 2 else norm(part)
        keep = jnp.sum(jnp.where(own, keeps[part * 8 : part * 8 + 8], 0.0), axis=0, keepdims=True)
        for side in range(2):
            gate = jnp.dot(wt_ref[side * 256 : side * 256 + 128, :], normed, preferred_element_type=F32)
            value = jnp.dot(wt_ref[side * 256 + 128 : side * 256 + 256, :], normed, preferred_element_type=F32)
            out = keep * sigmoid(gate) * value
            for kk_hi in range(3):
                at = side * 18 + part * 3 + kk_hi
                wide_ref[pl.ds(at, 128, stride=36), :] = out[:, kk_hi * 128 : kk_hi * 128 + 128]
        gate = sigmoid(lax.dot_general(normed, w_gate_ref[...], TN, preferred_element_type=F32))
        gate_ref[part * 8 : part * 8 + 8] = gate.reshape(3, 8, 16, 128).transpose(1, 0, 2, 3).reshape(8, 48, 128)
    out_ref[...] = wide_ref[...].astype(BF16)


def project(pair, mask, gain, bias, w_proj, w_gate):
    return pl.pallas_call(
        project_kernel,
        out_shape=(pltpu.VMEM((4608, 128), BF16), pltpu.VMEM((48, 48, 128), F32)),
        in_specs=[pl.BlockSpec(memory_space=pltpu.HBM)] * 6,
        out_specs=(pl.BlockSpec(memory_space=pltpu.VMEM), pl.BlockSpec(memory_space=pltpu.VMEM)),
        scratch_shapes=[
            pltpu.VMEM((48, 48, 128), F32),
            pltpu.VMEM((48, 48), jnp.int32),
            pltpu.VMEM((1, 128), F32),
            pltpu.VMEM((1, 128), F32),
            pltpu.VMEM((128, 512), BF16),
            pltpu.VMEM((128, 128), BF16),
            pltpu.VMEM((512, 128), BF16),
            pltpu.VMEM((6, 128, 384), BF16),
            pltpu.VMEM((4608, 128), F32),
            pltpu.SemaphoreType.DMA((11,)),
        ],
        compiler_params=pltpu.CompilerParams(vmem_limit_bytes=32 << 20),
        name="project",
    )(*(pltpu.with_memory_space_constraint(x, pltpu.HBM) for x in (pair, mask, gain, bias, w_proj, w_gate)))


def unmix(recv_ref, swap_ref, wide_ref, x_ref, dst_ref, side):
    wide_ref[...] = recv_ref[...].astype(F32)
    for s in range(18):
        for c in range(8):
            rows = wide_ref[rows_of(side * 18 + s, c, 36), :]
            x_ref[s * 16 : s * 16 + 16, c * 128 : c * 128 + 128] = rows.astype(BF16)
    for n in range(4):
        y = jnp.dot(x_ref[...], swap_ref[:, n * 256 : n * 256 + 256], preferred_element_type=F32).astype(BF16)
        for half in range(2):
            for s in range(18):
                at = (s // 3 * 8 + 2 * n + half) * 16
                lanes = slice(s % 3 * 128, s % 3 * 128 + 128)
                dst_ref[at : at + 16, lanes] = y[s * 16 : s * 16 + 16, half * 128 : half * 128 + 128]


def gather_left_kernel(recv_ref, swap_ref, out_ref, wide_ref, x_ref):
    unmix(recv_ref, swap_ref, wide_ref, x_ref, out_ref, 0)


def gather_right_kernel(core_ref, recv_ref, swap_ref, send_ref, keep_ref, wide_ref, x_ref, right_ref):
    unmix(recv_ref, swap_ref, wide_ref, x_ref, right_ref, 1)
    row = lax.broadcasted_iota(jnp.int32, (128, 256), 0)
    lane = lax.broadcasted_iota(jnp.int32, (128, 256), 1)
    b = row // 16
    for dst_ref, core in ((keep_ref, core_ref[0]), (send_ref, 1 - core_ref[0])):
        pick = (lane // 16 == row % 16) & (lane % 16 == b // 2 * 4 + core * 2 + b % 2)
        pick = pick.astype(F32).astype(BF16)
        for jj_hi in range(3):
            rows = jnp.dot(pick, right_ref[jj_hi * 256 : jj_hi * 256 + 256, :], preferred_element_type=F32)
            dst_ref[jj_hi * 128 : jj_hi * 128 + 128, :] = rows.astype(BF16)


UNMIX_SCRATCH = [pltpu.VMEM((4608, 128), F32), pltpu.VMEM((288, 1024), BF16)]


def gather_left(recv, swap):
    return pl.pallas_call(
        gather_left_kernel,
        out_shape=jax.ShapeDtypeStruct((768, 384), BF16),
        scratch_shapes=UNMIX_SCRATCH,
        compiler_params=pltpu.CompilerParams(vmem_limit_bytes=32 << 20),
        name="gather_left",
    )(recv, swap)


def gather_right(core, recv, swap):
    vmem = pl.BlockSpec(memory_space=pltpu.VMEM)
    half = jax.ShapeDtypeStruct((384, 384), BF16)
    return pl.pallas_call(
        gather_right_kernel,
        out_shape=(half, half),
        in_specs=[pl.BlockSpec(memory_space=pltpu.SMEM), vmem, vmem],
        out_specs=(vmem, vmem),
        scratch_shapes=UNMIX_SCRATCH + [pltpu.VMEM((768, 384), BF16)],
        compiler_params=pltpu.CompilerParams(vmem_limit_bytes=32 << 20),
        name="gather_right",
    )(core, recv, swap)


def contract_own_kernel(left_ref, right_ref, out_ref):
    for i in range(6):
        rows = slice(i * 128, i * 128 + 128)
        out_ref[rows, :] = lax.dot_general(left_ref[rows, :], right_ref[...], NT, preferred_element_type=F32)


def contract_own(left, right):
    return pl.pallas_call(
        contract_own_kernel,
        out_shape=jax.ShapeDtypeStruct((768, 384), F32),
        compiler_params=pltpu.CompilerParams(vmem_limit_bytes=32 << 20),
        cost_estimate=pl.CostEstimate(flops=2 * 768 * 384 * 384, bytes_accessed=2_000_000, transcendentals=0),
        name="contract_own",
    )(left, right)


def contract_kernel(own_ref, left_ref, right_ref, swap_ref, out_ref, x_ref, wide_ref):
    for i in range(6):
        rows = slice(i * 128, i * 128 + 128)
        mixed = lax.dot_general(left_ref[rows, :], right_ref[...], NT, preferred_element_type=F32)
        mixed = (own_ref[rows, :] + mixed).astype(BF16)
        for j in range(3):
            for a in range(8):
                at = (i * 3 + j) * 16
                x_ref[at : at + 16, a * 128 : a * 128 + 128] = mixed[a * 16 : a * 16 + 16, j * 128 : j * 128 + 128]
    for n in range(4):
        y = jnp.dot(x_ref[...], swap_ref[:, n * 256 : n * 256 + 256], preferred_element_type=F32)
        for half in range(2):
            for s in range(18):
                wide_ref[rows_of(s, 2 * n + half, 18), :] = y[s * 16 : s * 16 + 16, half * 128 : half * 128 + 128]
    out_ref[...] = wide_ref[...].astype(BF16)


def contract(own, left, right, swap):
    return pl.pallas_call(
        contract_kernel,
        out_shape=jax.ShapeDtypeStruct((2304, 128), BF16),
        scratch_shapes=[pltpu.VMEM((288, 1024), BF16), pltpu.VMEM((2304, 128), F32)],
        compiler_params=pltpu.CompilerParams(vmem_limit_bytes=32 << 20),
        name="contract",
    )(own, left, right, swap)


def finish_kernel(mixed_ref, gate_ref, gain_ref, bias_ref, w_ref, out_hbm, wide_ref, out_ref, sems):
    wide_ref[...] = mixed_ref[...].astype(F32)
    gain, bias = column(gain_ref[...]), column(bias_ref[...])
    copies = []
    for part in range(6):
        for jj_hi in range(3):
            mixed = wide_ref[pl.ds(part * 3 + jj_hi, 128, stride=18), :]
            normed = layer_norm(mixed, gain, bias, 0).astype(BF16)
            projected = lax.dot_general(normed, w_ref[...], TN, preferred_element_type=F32).reshape(8, 16, 128)
            rows, cols = slice(part * 8, part * 8 + 8), slice(jj_hi * 16, jj_hi * 16 + 16)
            out_ref[rows, cols, :] = gate_ref[rows, cols, :] * projected
        rows = pl.ds(part * 8, 8)
        copies.append(pltpu.make_async_copy(out_ref.at[rows], out_hbm.at[rows], sems.at[part]))
        copies[-1].start()
    for copy in copies:
        copy.wait()


def finish(mixed, gate, gain, bias, w_out):
    return pl.pallas_call(
        finish_kernel,
        out_shape=jax.ShapeDtypeStruct((48, 48, 128), F32),
        in_specs=[pl.BlockSpec(memory_space=pltpu.VMEM)] * 5,
        out_specs=pl.BlockSpec(memory_space=pltpu.HBM),
        scratch_shapes=[pltpu.VMEM((2304, 128), F32), pltpu.VMEM((48, 48, 128), F32), pltpu.SemaphoreType.DMA((6,))],
        compiler_params=pltpu.CompilerParams(vmem_limit_bytes=32 << 20),
        name="finish",
    )(mixed, gate, gain, bias, w_out)


def exchange(messages):
    rows = messages.shape[0] // 128
    tiles = messages.reshape(128, 9, rows // 9, 128)
    return lax.all_to_all(tiles, GROUP, 0, 0, tiled=True).reshape(128 * rows, 128)


def per_device(pair, pair_mask, ln_gain, ln_bias, w_proj, w_gate, out_gain, out_bias, w_out):
    hold = lax.optimization_barrier
    sent, gate = project(pair, pair_mask, ln_gain.reshape(1, 128), ln_bias.reshape(1, 128), w_proj, w_gate)
    core = lax.axis_index("core").astype(jnp.int32).reshape(1)
    sent, gate, core = hold((sent, gate, core))
    recv, gate, w_out, out_gain, out_bias = hold((exchange(sent), gate, w_out, out_gain, out_bias))
    place = np.arange(1024)
    swap = jnp.asarray(place[None, :] == (place // 16 % 8 * 128 + place // 128 * 16 + place % 16)[:, None], BF16)
    swap_cores = lambda v: lax.ppermute(v, "core", [(0, 1), (1, 0)])
    left = gather_left(recv, swap)
    left2 = swap_cores(left)
    right_send, right = gather_right(core, recv, swap)
    right2 = swap_cores(right_send)
    own = contract_own(left, right)
    sent = contract(own, left2, right2, swap)
    sent, gate, w_out, out_gain, out_bias = hold((sent, gate, w_out, out_gain, out_bias))
    mixed, gate, w_out, out_gain, out_bias = hold((exchange(sent), gate, w_out, out_gain, out_bias))
    return finish(mixed, gate, out_gain.reshape(1, 128), out_bias.reshape(1, 128), w_out)


def solution(mesh):
    fine = Mesh(mesh.devices.reshape(2, 4, 2, 2, 4, 2), ROW + COL)
    return jax.shard_map(
        per_device,
        mesh=fine,
        in_specs=(P(ROW, COL, None), P(ROW, COL), P(), P(), P(), P(), P(), P(), P()),
        out_specs=P(ROW, COL, None),
        check_vma=False,
    )
```

```python
import math

import jax
import jax.numpy as jnp
import numpy as np
from jax import lax
from jax.experimental import pallas as pl
from jax.experimental.pallas import tpu as pltpu
from jax.sharding import Mesh, PartitionSpec as P

EPS = 1e-05
ROW = ("xh", "zh", "zl")
COL = ("xl", "y", "core")
GROUP = ('zl', 'y', 'zh', 'xh', 'xl')
SIZES = dict(zh=4, zl=2, xl=2, y=4, xh=2)
STEP = {axis: math.prod(SIZES[later] for later in GROUP[n + 1 :]) for n, axis in enumerate(GROUP)}
XH_FIRST = GROUP.index("xh") < GROUP.index("zh")
B_STEP = STEP["zh" if XH_FIRST else "xh"]
PAIR = [STEP["y"] * (c % 4 if XH_FIRST else c // 2) + STEP["xl"] * (c // 4 if XH_FIRST else c % 2) for c in range(8)]
F32, BF16 = jnp.float32, jnp.bfloat16
NT = (((1,), (1,)), ((), ()))
TN = (((0,), (0,)), ((), ()))


def sigmoid(x):
    return 0.5 * jnp.tanh(0.5 * x) + 0.5


def layer_norm(x, gain, bias, axis):
    mean = jnp.mean(x, axis=axis, keepdims=True)
    centred = x - mean
    var = jnp.mean(centred * centred, axis=axis, keepdims=True)
    return centred * lax.rsqrt(var + EPS) * gain + bias


def column(row):
    return jnp.broadcast_to(row, (8, 128)).T[:, :1]


def full(*shape):
    return pl.BlockSpec(shape, lambda i: (0,) * len(shape))


def rows_of(at, pair, zl, rows):
    return pl.ds((PAIR[pair] + STEP["zl"] * zl) * rows + at, 8, stride=B_STEP * rows)


def project_kernel(
    pair_hbm, mask_hbm, gain_hbm, bias_hbm, w_hbm, w_gate_hbm, out_ref, gate_ref,
    pair_ref, mask_ref, gain_ref, bias_ref, w_ref, w_gate_ref, wt_ref, normed_ref, wide_ref, sems,
):
    small = [
        pltpu.make_async_copy(src, dst, sems.at[6 + n])
        for n, (src, dst) in enumerate(
            (
                (w_hbm, w_ref),
                (gain_hbm, gain_ref),
                (bias_hbm, bias_ref),
                (mask_hbm, mask_ref),
                (w_gate_hbm, w_gate_ref),
            )
        )
    ]
    chunks = [
        pltpu.make_async_copy(pair_hbm.at[pl.ds(part * 8, 8)], pair_ref.at[pl.ds(part * 8, 8)], sems.at[part])
        for part in range(6)
    ]
    for copy in chunks[:2] + small + chunks[2:]:
        copy.start()
    lane = lax.broadcasted_iota(jnp.int32, (48, 384), 1)
    row = lax.broadcasted_iota(jnp.int32, (48, 384), 0)
    spread = (lane // 128 * 16 + lane % 16 == row).astype(F32).astype(BF16)
    own = lax.broadcasted_iota(jnp.int32, (8, 384), 1) // 16 % 8 == lax.broadcasted_iota(jnp.int32, (8, 384), 0)
    for copy in small + chunks[:2]:
        copy.wait()
    wt_ref[...] = w_ref[...].astype(F32).T.astype(BF16)
    keeps = jnp.dot(mask_ref[...].astype(F32).astype(BF16), spread, preferred_element_type=F32)
    gain, bias = column(gain_ref[...]), column(bias_ref[...])

    def norm(part):
        x = pair_ref[part * 8 : part * 8 + 8].reshape(8, 3, 16, 128).transpose(1, 0, 2, 3).reshape(384, 128)
        return layer_norm(x.T, gain, bias, 0).astype(BF16)

    for part in range(2):
        normed_ref[part] = norm(part)
    for copy in chunks[2:]:
        copy.wait()
    for part in range(6):
        normed = normed_ref[part] if part < 2 else norm(part)
        keep = jnp.sum(jnp.where(own, keeps[part * 8 : part * 8 + 8], 0.0), axis=0, keepdims=True)
        for side in range(2):
            gate = jnp.dot(wt_ref[side * 256 : side * 256 + 128, :], normed, preferred_element_type=F32)
            value = jnp.dot(wt_ref[side * 256 + 128 : side * 256 + 256, :], normed, preferred_element_type=F32)
            out = keep * sigmoid(gate) * value
            for kk_hi in range(3):
                at = side * 18 + part * 3 + kk_hi
                wide_ref[pl.ds(at, 128, stride=36), :] = out[:, kk_hi * 128 : kk_hi * 128 + 128]
        gate = sigmoid(lax.dot_general(normed, w_gate_ref[...], TN, preferred_element_type=F32))
        gate_ref[part * 8 : part * 8 + 8] = gate.reshape(3, 8, 16, 128).transpose(1, 0, 2, 3).reshape(8, 48, 128)
    out_ref[...] = wide_ref[...].astype(BF16)


def project(pair, mask, gain, bias, w_proj, w_gate):
    return pl.pallas_call(
        project_kernel,
        out_shape=(pltpu.VMEM((4608, 128), BF16), pltpu.VMEM((48, 48, 128), F32)),
        in_specs=[pl.BlockSpec(memory_space=pltpu.HBM)] * 6,
        out_specs=(pl.BlockSpec(memory_space=pltpu.VMEM), pl.BlockSpec(memory_space=pltpu.VMEM)),
        scratch_shapes=[
            pltpu.VMEM((48, 48, 128), F32),
            pltpu.VMEM((48, 48), jnp.int32),
            pltpu.VMEM((1, 128), F32),
            pltpu.VMEM((1, 128), F32),
            pltpu.VMEM((128, 512), BF16),
            pltpu.VMEM((128, 128), BF16),
            pltpu.VMEM((512, 128), BF16),
            pltpu.VMEM((6, 128, 384), BF16),
            pltpu.VMEM((4608, 128), F32),
            pltpu.SemaphoreType.DMA((11,)),
        ],
        compiler_params=pltpu.CompilerParams(vmem_limit_bytes=32 << 20),
        name="project",
    )(*(pltpu.with_memory_space_constraint(x, pltpu.HBM) for x in (pair, mask, gain, bias, w_proj, w_gate)))


def gather_left_kernel(recv_ref, swap_ref, out_ref, wide_ref, x_ref):
    wide_ref[...] = recv_ref[...].astype(F32)
    for s in range(18):
        for c in range(8):
            rows = [wide_ref[rows_of(s, c, zl, 36), :] for zl in range(2)]
            x_ref[s * 16 : s * 16 + 16, c * 128 : c * 128 + 128] = jnp.concatenate(rows).astype(BF16)
    for n in range(4):
        y = jnp.dot(x_ref[...], swap_ref[:, n * 256 : n * 256 + 256], preferred_element_type=F32).astype(BF16)
        for half in range(2):
            for s in range(18):
                at = (s // 3 * 8 + 2 * n + half) * 16
                lanes = slice(s % 3 * 128, s % 3 * 128 + 128)
                out_ref[at : at + 16, lanes] = y[s * 16 : s * 16 + 16, half * 128 : half * 128 + 128]


def gather_right_kernel(of_ref, recv_ref, swap_ref, out_ref, wide_ref, x_ref, rows_ref):
    wide_ref[...] = recv_ref[...].astype(F32)
    for s in range(0, 18, 2):
        for c in range(8):
            rows = [wide_ref[rows_of(18 + s + k, c, of_ref[0], 36), :] for k in range(2)]
            x_ref[s * 8 : s * 8 + 16, c * 128 : c * 128 + 128] = jnp.concatenate(rows).astype(BF16)
    for n in range(4):
        y = jnp.dot(x_ref[...], swap_ref[:, n * 256 : n * 256 + 256], preferred_element_type=F32)
        for half in range(2):
            for s in range(18):
                at = (s // 3 * 8 + 2 * n + half) * 8
                rows_ref[s % 3, at : at + 8, :] = y[s * 8 : s * 8 + 8, half * 128 : half * 128 + 128]
    for kk_hi in range(3):
        for jj_hi in range(3):
            for b in range(8):
                at = (jj_hi * 8 + b) * 16
                rows = rows_ref[kk_hi, pl.ds(jj_hi * 128 + b, 16, stride=8), :]
                out_ref[at : at + 16, kk_hi * 128 : kk_hi * 128 + 128] = rows.astype(BF16)


def gather_left(recv, swap):
    return pl.pallas_call(
        gather_left_kernel,
        out_shape=jax.ShapeDtypeStruct((768, 384), BF16),
        scratch_shapes=[pltpu.VMEM((4608, 128), F32), pltpu.VMEM((288, 1024), BF16)],
        compiler_params=pltpu.CompilerParams(vmem_limit_bytes=32 << 20),
        name="gather_left",
    )(recv, swap)


def gather_right(of, recv, swap):
    vmem = pl.BlockSpec(memory_space=pltpu.VMEM)
    return pl.pallas_call(
        gather_right_kernel,
        out_shape=jax.ShapeDtypeStruct((384, 384), BF16),
        in_specs=[pl.BlockSpec(memory_space=pltpu.SMEM), vmem, vmem],
        out_specs=vmem,
        scratch_shapes=[pltpu.VMEM((4608, 128), F32), pltpu.VMEM((144, 1024), BF16), pltpu.VMEM((3, 384, 128), F32)],
        compiler_params=pltpu.CompilerParams(vmem_limit_bytes=32 << 20),
        name="gather_right",
    )(of, recv, swap)


def contract_own_kernel(left_ref, right_ref, out_ref):
    for i in range(6):
        rows = slice(i * 128, i * 128 + 128)
        out_ref[rows, :] = lax.dot_general(left_ref[rows, :], right_ref[...], NT, preferred_element_type=F32)


def contract_own(left, right):
    return pl.pallas_call(
        contract_own_kernel,
        out_shape=jax.ShapeDtypeStruct((768, 384), F32),
        compiler_params=pltpu.CompilerParams(vmem_limit_bytes=32 << 20),
        cost_estimate=pl.CostEstimate(flops=2 * 768 * 384 * 384, bytes_accessed=2_000_000, transcendentals=0),
        name="contract_own",
    )(left, right)


def contract_kernel(own_ref, left_ref, right_ref, swap_ref, out_ref, x_ref, wide_ref):
    for i in range(6):
        rows = slice(i * 128, i * 128 + 128)
        mixed = lax.dot_general(left_ref[rows, :], right_ref[...], NT, preferred_element_type=F32)
        mixed = (own_ref[rows, :] + mixed).astype(BF16)
        for j in range(3):
            for a in range(8):
                at = (i * 3 + j) * 16
                x_ref[at : at + 16, a * 128 : a * 128 + 128] = mixed[a * 16 : a * 16 + 16, j * 128 : j * 128 + 128]
    for n in range(4):
        y = jnp.dot(x_ref[...], swap_ref[:, n * 256 : n * 256 + 256], preferred_element_type=F32)
        for half in range(2):
            for s in range(18):
                for zl in range(2):
                    at = s * 16 + zl * 8
                    wide_ref[rows_of(s, 2 * n + half, zl, 18), :] = y[at : at + 8, half * 128 : half * 128 + 128]
    out_ref[...] = wide_ref[...].astype(BF16)


def contract(own, left, right, swap):
    return pl.pallas_call(
        contract_kernel,
        out_shape=jax.ShapeDtypeStruct((2304, 128), BF16),
        scratch_shapes=[pltpu.VMEM((288, 1024), BF16), pltpu.VMEM((2304, 128), F32)],
        compiler_params=pltpu.CompilerParams(vmem_limit_bytes=32 << 20),
        name="contract",
    )(own, left, right, swap)


def finish_kernel(mixed_ref, gate_ref, gain_ref, bias_ref, w_ref, out_hbm, wide_ref, out_ref, sems):
    wide_ref[...] = mixed_ref[...].astype(F32)
    gain, bias = column(gain_ref[...]), column(bias_ref[...])
    copies = []
    for part in range(6):
        for jj_hi in range(3):
            mixed = wide_ref[pl.ds(part * 3 + jj_hi, 128, stride=18), :]
            normed = layer_norm(mixed, gain, bias, 0).astype(BF16)
            projected = lax.dot_general(normed, w_ref[...], TN, preferred_element_type=F32).reshape(8, 16, 128)
            rows, cols = slice(part * 8, part * 8 + 8), slice(jj_hi * 16, jj_hi * 16 + 16)
            out_ref[rows, cols, :] = gate_ref[rows, cols, :] * projected
        rows = pl.ds(part * 8, 8)
        copies.append(pltpu.make_async_copy(out_ref.at[rows], out_hbm.at[rows], sems.at[part]))
        copies[-1].start()
    for copy in copies:
        copy.wait()


def finish(mixed, gate, gain, bias, w_out):
    return pl.pallas_call(
        finish_kernel,
        out_shape=jax.ShapeDtypeStruct((48, 48, 128), F32),
        in_specs=[pl.BlockSpec(memory_space=pltpu.VMEM)] * 5,
        out_specs=pl.BlockSpec(memory_space=pltpu.HBM),
        scratch_shapes=[pltpu.VMEM((2304, 128), F32), pltpu.VMEM((48, 48, 128), F32), pltpu.SemaphoreType.DMA((6,))],
        compiler_params=pltpu.CompilerParams(vmem_limit_bytes=32 << 20),
        name="finish",
    )(mixed, gate, gain, bias, w_out)


def exchange(messages):
    rows = messages.shape[0] // 128
    tiles = messages.reshape(128, 9, rows // 9, 128)
    return lax.all_to_all(tiles, GROUP, 0, 0, tiled=True).reshape(128 * rows, 128)


def per_device(pair, pair_mask, ln_gain, ln_bias, w_proj, w_gate, out_gain, out_bias, w_out):
    hold = lax.optimization_barrier
    sent, gate = project(pair, pair_mask, ln_gain.reshape(1, 128), ln_bias.reshape(1, 128), w_proj, w_gate)
    core = lax.axis_index("core").astype(jnp.int32).reshape(1)
    sent, gate, core, other = hold((sent, gate, core, 1 - core))
    recv, gate, w_out, out_gain, out_bias = hold((exchange(sent), gate, w_out, out_gain, out_bias))
    place = np.arange(1024)
    swap = jnp.asarray(place[None, :] == (place // 16 % 8 * 128 + place // 128 * 16 + place % 16)[:, None], BF16)
    swap_cores = lambda v: lax.ppermute(v, "core", [(0, 1), (1, 0)])
    left = gather_left(recv, swap)
    left2 = swap_cores(left)
    right2 = swap_cores(gather_right(other, recv, swap))
    right = gather_right(core, recv, swap)
    own = contract_own(left, right)
    sent = contract(own, left2, right2, swap)
    sent, gate, w_out, out_gain, out_bias = hold((sent, gate, w_out, out_gain, out_bias))
    mixed, gate, w_out, out_gain, out_bias = hold((exchange(sent), gate, w_out, out_gain, out_bias))
    return finish(mixed, gate, out_gain.reshape(1, 128), out_bias.reshape(1, 128), w_out)


def solution(mesh):
    fine = Mesh(mesh.devices.reshape(2, 4, 2, 2, 4, 2), ROW + COL)
    return jax.shard_map(
        per_device,
        mesh=fine,
        in_specs=(P(ROW, COL, None), P(ROW, COL), P(), P(), P(), P(), P(), P(), P()),
        out_specs=P(ROW, COL, None),
        check_vma=False,
    )
```

```python
import math

import jax
import jax.numpy as jnp
import numpy as np
from jax import lax
from jax.experimental import pallas as pl
from jax.experimental.pallas import tpu as pltpu
from jax.sharding import Mesh, PartitionSpec as P

EPS = 1e-05
ROW = ("xh", "zh", "zl")
COL = ("xl", "y", "core")
GROUP = ("zl", "y", "zh", "xh", "xl")
SIZES = dict(zh=4, zl=2, xl=2, y=4, xh=2)
STEP = {axis: math.prod(SIZES[later] for later in GROUP[n + 1 :]) for n, axis in enumerate(GROUP)}
XH_FIRST = GROUP.index("xh") < GROUP.index("zh")
B_STEP = STEP["zh" if XH_FIRST else "xh"]
PAIR = [STEP["y"] * (c % 4 if XH_FIRST else c // 2) + STEP["xl"] * (c // 4 if XH_FIRST else c % 2) for c in range(8)]
F32, BF16 = jnp.float32, jnp.bfloat16
SPARE = 128
NT = (((1,), (1,)), ((), ()))
TN = (((0,), (0,)), ((), ()))


def sigmoid(x):
    return 0.5 * jnp.tanh(0.5 * x) + 0.5


def layer_norm(x, gain, bias, axis):
    mean = jnp.mean(x, axis=axis, keepdims=True)
    centred = x - mean
    var = jnp.mean(centred * centred, axis=axis, keepdims=True)
    return centred * lax.rsqrt(var + EPS) * gain + bias


def column(row):
    return jnp.broadcast_to(row, (8, 128)).T[:, :1]


def full(*shape):
    return pl.BlockSpec(shape, lambda i: (0,) * len(shape))


def rows_of(at, pair, zl, rows):
    return pl.ds((PAIR[pair] + STEP["zl"] * zl) * rows + at, 8, stride=B_STEP * rows)


def project_kernel(
    pair_hbm, mask_hbm, gain_hbm, bias_hbm, w_hbm, w_gate_hbm, out_ref, gate_ref,
    pair_ref, mask_ref, gain_ref, bias_ref, w_ref, w_gate_ref, wt_ref, normed_ref, wide_ref, sems,
):
    small = [
        pltpu.make_async_copy(src, dst, sems.at[6 + n])
        for n, (src, dst) in enumerate(
            (
                (w_hbm, w_ref),
                (gain_hbm, gain_ref),
                (bias_hbm, bias_ref),
                (mask_hbm, mask_ref),
                (w_gate_hbm, w_gate_ref),
            )
        )
    ]
    chunks = [
        pltpu.make_async_copy(pair_hbm.at[pl.ds(part * 8, 8)], pair_ref.at[pl.ds(part * 8, 8)], sems.at[part])
        for part in range(6)
    ]
    for copy in chunks[:2] + small + chunks[2:]:
        copy.start()
    lane = lax.broadcasted_iota(jnp.int32, (48, 384), 1)
    row = lax.broadcasted_iota(jnp.int32, (48, 384), 0)
    spread = (lane // 128 * 16 + lane % 16 == row).astype(F32).astype(BF16)
    own = lax.broadcasted_iota(jnp.int32, (8, 384), 1) // 16 % 8 == lax.broadcasted_iota(jnp.int32, (8, 384), 0)
    for copy in small + chunks[:2]:
        copy.wait()
    wt_ref[...] = w_ref[...].astype(F32).T.astype(BF16)
    keeps = jnp.dot(mask_ref[...].astype(F32).astype(BF16), spread, preferred_element_type=F32)
    gain, bias = column(gain_ref[...]), column(bias_ref[...])

    def norm(part):
        x = pair_ref[part * 8 : part * 8 + 8].reshape(8, 3, 16, 128).transpose(1, 0, 2, 3).reshape(384, 128)
        return layer_norm(x.T, gain, bias, 0).astype(BF16)

    for part in range(2):
        normed_ref[part] = norm(part)
    for copy in chunks[2:]:
        copy.wait()
    for part in range(6):
        normed = normed_ref[part] if part < 2 else norm(part)
        keep = jnp.sum(jnp.where(own, keeps[part * 8 : part * 8 + 8], 0.0), axis=0, keepdims=True)
        for side in range(2):
            gate = jnp.dot(wt_ref[side * 256 : side * 256 + 128, :], normed, preferred_element_type=F32)
            value = jnp.dot(wt_ref[side * 256 + 128 : side * 256 + 256, :], normed, preferred_element_type=F32)
            out = keep * sigmoid(gate) * value
            for kk_hi in range(3):
                at = side * 18 + part * 3 + kk_hi
                wide_ref[pl.ds(at, 128, stride=36), :] = out[:, kk_hi * 128 : kk_hi * 128 + 128]
        gate = sigmoid(lax.dot_general(normed, w_gate_ref[...], TN, preferred_element_type=F32))
        gate_ref[part * 8 : part * 8 + 8] = gate.reshape(3, 8, 16, 128).transpose(1, 0, 2, 3).reshape(8, 48, 128)
    out_ref[...] = wide_ref[:4608, :].astype(BF16)


def project(pair, mask, gain, bias, w_proj, w_gate):
    return pl.pallas_call(
        project_kernel,
        out_shape=(pltpu.VMEM((4608, 128), BF16), pltpu.VMEM((48, 48, 128), F32)),
        in_specs=[pl.BlockSpec(memory_space=pltpu.HBM)] * 6,
        out_specs=(pl.BlockSpec(memory_space=pltpu.VMEM), pl.BlockSpec(memory_space=pltpu.VMEM)),
        scratch_shapes=[
            pltpu.VMEM((48, 48, 128), F32),
            pltpu.VMEM((48, 48), jnp.int32),
            pltpu.VMEM((1, 128), F32),
            pltpu.VMEM((1, 128), F32),
            pltpu.VMEM((128, 512), BF16),
            pltpu.VMEM((128, 128), BF16),
            pltpu.VMEM((512, 128), BF16),
            pltpu.VMEM((6, 128, 384), BF16),
            pltpu.VMEM((4608 + SPARE, 128), F32),
            pltpu.SemaphoreType.DMA((11,)),
        ],
        compiler_params=pltpu.CompilerParams(vmem_limit_bytes=32 << 20),
        name="project",
    )(*(pltpu.with_memory_space_constraint(x, pltpu.HBM) for x in (pair, mask, gain, bias, w_proj, w_gate)))


def gather_left_kernel(recv_ref, swap_ref, out_ref, wide_ref, x_ref):
    wide_ref[:4608, :] = recv_ref[...].astype(F32)
    for s in range(18):
        for c in range(8):
            rows = [wide_ref[rows_of(s, c, zl, 36), :] for zl in range(2)]
            x_ref[s * 16 : s * 16 + 16, c * 128 : c * 128 + 128] = jnp.concatenate(rows).astype(BF16)
    for n in range(4):
        y = jnp.dot(x_ref[...], swap_ref[:, n * 256 : n * 256 + 256], preferred_element_type=F32).astype(BF16)
        for half in range(2):
            for s in range(18):
                at = (s // 3 * 8 + 2 * n + half) * 16
                lanes = slice(s % 3 * 128, s % 3 * 128 + 128)
                out_ref[at : at + 16, lanes] = y[s * 16 : s * 16 + 16, half * 128 : half * 128 + 128]


def gather_right_kernel(of_ref, recv_ref, swap_ref, out_ref, wide_ref, x_ref, rows_ref):
    wide_ref[:2304, :] = recv_ref[pl.ds(pl.multiple_of(of_ref[0] * 2304, 2304), 2304), :].astype(F32)
    for s in range(0, 18, 2):
        for c in range(8):
            rows = [wide_ref[rows_of(18 + s + k, c, 0, 36), :] for k in range(2)]
            x_ref[s * 8 : s * 8 + 16, c * 128 : c * 128 + 128] = jnp.concatenate(rows).astype(BF16)
    for n in range(4):
        y = jnp.dot(x_ref[...], swap_ref[:, n * 256 : n * 256 + 256], preferred_element_type=F32)
        for half in range(2):
            for s in range(18):
                at = (s // 3 * 8 + 2 * n + half) * 8
                rows_ref[s % 3, at : at + 8, :] = y[s * 8 : s * 8 + 8, half * 128 : half * 128 + 128]
    for kk_hi in range(3):
        for jj_hi in range(3):
            for b in range(8):
                at = (jj_hi * 8 + b) * 16
                rows = rows_ref[kk_hi, pl.ds(jj_hi * 128 + b, 16, stride=8), :]
                out_ref[at : at + 16, kk_hi * 128 : kk_hi * 128 + 128] = rows.astype(BF16)


def gather_left(recv, swap):
    return pl.pallas_call(
        gather_left_kernel,
        out_shape=jax.ShapeDtypeStruct((768, 384), BF16),
        scratch_shapes=[pltpu.VMEM((4608 + SPARE, 128), F32), pltpu.VMEM((288, 1024), BF16)],
        compiler_params=pltpu.CompilerParams(vmem_limit_bytes=32 << 20),
        name="gather_left",
    )(recv, swap)


def gather_right(of, recv, swap):
    vmem = pl.BlockSpec(memory_space=pltpu.VMEM)
    return pl.pallas_call(
        gather_right_kernel,
        out_shape=jax.ShapeDtypeStruct((384, 384), BF16),
        in_specs=[pl.BlockSpec(memory_space=pltpu.SMEM), vmem, vmem],
        out_specs=vmem,
        scratch_shapes=[
            pltpu.VMEM((2304 + SPARE, 128), F32),
            pltpu.VMEM((144, 1024), BF16),
            pltpu.VMEM((3, 384 + SPARE, 128), F32),
        ],
        compiler_params=pltpu.CompilerParams(vmem_limit_bytes=32 << 20),
        name="gather_right",
    )(of, recv, swap)


def contract_own_kernel(left_ref, right_ref, out_ref):
    for i in range(6):
        rows = slice(i * 128, i * 128 + 128)
        out_ref[rows, :] = lax.dot_general(left_ref[rows, :], right_ref[...], NT, preferred_element_type=F32)


def contract_own(left, right):
    return pl.pallas_call(
        contract_own_kernel,
        out_shape=jax.ShapeDtypeStruct((768, 384), F32),
        compiler_params=pltpu.CompilerParams(vmem_limit_bytes=32 << 20),
        cost_estimate=pl.CostEstimate(flops=2 * 768 * 384 * 384, bytes_accessed=2_000_000, transcendentals=0),
        name="contract_own",
    )(left, right)


def contract_kernel(own_ref, left_ref, right_ref, swap_ref, out_ref, x_ref, wide_ref):
    for i in range(6):
        rows = slice(i * 128, i * 128 + 128)
        mixed = lax.dot_general(left_ref[rows, :], right_ref[...], NT, preferred_element_type=F32)
        mixed = (own_ref[rows, :] + mixed).astype(BF16)
        for j in range(3):
            for a in range(8):
                at = (i * 3 + j) * 16
                x_ref[at : at + 16, a * 128 : a * 128 + 128] = mixed[a * 16 : a * 16 + 16, j * 128 : j * 128 + 128]
    for n in range(4):
        y = jnp.dot(x_ref[...], swap_ref[:, n * 256 : n * 256 + 256], preferred_element_type=F32)
        for half in range(2):
            for s in range(18):
                for zl in range(2):
                    at = s * 16 + zl * 8
                    wide_ref[rows_of(s, 2 * n + half, zl, 18), :] = y[at : at + 8, half * 128 : half * 128 + 128]
    out_ref[...] = wide_ref[:2304, :].astype(BF16)


def contract(own, left, right, swap):
    return pl.pallas_call(
        contract_kernel,
        out_shape=jax.ShapeDtypeStruct((2304, 128), BF16),
        scratch_shapes=[pltpu.VMEM((288, 1024), BF16), pltpu.VMEM((2304 + SPARE, 128), F32)],
        compiler_params=pltpu.CompilerParams(vmem_limit_bytes=32 << 20),
        name="contract",
    )(own, left, right, swap)


def finish_kernel(mixed_ref, gate_ref, gain_ref, bias_ref, w_ref, out_hbm, wide_ref, out_ref, sems):
    wide_ref[:2304, :] = mixed_ref[...].astype(F32)
    gain, bias = column(gain_ref[...]), column(bias_ref[...])
    copies = []
    for part in range(6):
        for jj_hi in range(3):
            mixed = wide_ref[pl.ds(part * 3 + jj_hi, 128, stride=18), :]
            normed = layer_norm(mixed, gain, bias, 0).astype(BF16)
            projected = lax.dot_general(normed, w_ref[...], TN, preferred_element_type=F32).reshape(8, 16, 128)
            rows, cols = slice(part * 8, part * 8 + 8), slice(jj_hi * 16, jj_hi * 16 + 16)
            out_ref[rows, cols, :] = gate_ref[rows, cols, :] * projected
        rows = pl.ds(part * 8, 8)
        copies.append(pltpu.make_async_copy(out_ref.at[rows], out_hbm.at[rows], sems.at[part]))
        copies[-1].start()
    for copy in copies:
        copy.wait()


def finish(mixed, gate, gain, bias, w_out):
    return pl.pallas_call(
        finish_kernel,
        out_shape=jax.ShapeDtypeStruct((48, 48, 128), F32),
        in_specs=[pl.BlockSpec(memory_space=pltpu.VMEM)] * 5,
        out_specs=pl.BlockSpec(memory_space=pltpu.HBM),
        scratch_shapes=[
            pltpu.VMEM((2304 + SPARE, 128), F32),
            pltpu.VMEM((48, 48, 128), F32),
            pltpu.SemaphoreType.DMA((6,)),
        ],
        compiler_params=pltpu.CompilerParams(vmem_limit_bytes=32 << 20),
        name="finish",
    )(mixed, gate, gain, bias, w_out)


def exchange(messages):
    rows = messages.shape[0] // 128
    tiles = messages.reshape(128, 9, rows // 9, 128)
    return lax.all_to_all(tiles, GROUP, 0, 0, tiled=True).reshape(128 * rows, 128)


def per_device(pair, pair_mask, ln_gain, ln_bias, w_proj, w_gate, out_gain, out_bias, w_out):
    hold = lax.optimization_barrier
    sent, gate = project(pair, pair_mask, ln_gain.reshape(1, 128), ln_bias.reshape(1, 128), w_proj, w_gate)
    core = lax.axis_index("core").astype(jnp.int32).reshape(1)
    sent, gate, core, other = hold((sent, gate, core, 1 - core))
    recv, gate, w_out, out_gain, out_bias = hold((exchange(sent), gate, w_out, out_gain, out_bias))
    place = np.arange(1024)
    swap = jnp.asarray(place[None, :] == (place // 16 % 8 * 128 + place // 128 * 16 + place % 16)[:, None], BF16)
    swap_cores = lambda v: lax.ppermute(v, "core", [(0, 1), (1, 0)])
    left = gather_left(recv, swap)
    left2 = swap_cores(left)
    right2 = swap_cores(gather_right(other, recv, swap))
    right = gather_right(core, recv, swap)
    own = contract_own(left, right)
    sent = contract(own, left2, right2, swap)
    sent, gate, w_out, out_gain, out_bias = hold((sent, gate, w_out, out_gain, out_bias))
    mixed, gate, w_out, out_gain, out_bias = hold((exchange(sent), gate, w_out, out_gain, out_bias))
    return finish(mixed, gate, out_gain.reshape(1, 128), out_bias.reshape(1, 128), w_out)


def solution(mesh):
    fine = Mesh(mesh.devices.reshape(2, 4, 2, 2, 4, 2), ROW + COL)
    return jax.shard_map(
        per_device,
        mesh=fine,
        in_specs=(P(ROW, COL, None), P(ROW, COL), P(), P(), P(), P(), P(), P(), P()),
        out_specs=P(ROW, COL, None),
        check_vma=False,
    )
```

```python
import math

import jax
import jax.numpy as jnp
import numpy as np
from jax import lax
from jax.experimental import pallas as pl
from jax.experimental.pallas import tpu as pltpu
from jax.sharding import Mesh, PartitionSpec as P

EPS = 1e-05
ROW = ("xh", "zh", "zl")
COL = ("xl", "y", "core")
GROUP = ("zl", "y", "zh", "xh", "xl")
SIZES = dict(zh=4, zl=2, xl=2, y=4, xh=2)
STEP = {axis: math.prod(SIZES[later] for later in GROUP[n + 1 :]) for n, axis in enumerate(GROUP)}
XH_FIRST = GROUP.index("xh") < GROUP.index("zh")
B_STEP = STEP["zh" if XH_FIRST else "xh"]
PAIR = [STEP["y"] * (c % 4 if XH_FIRST else c // 2) + STEP["xl"] * (c // 4 if XH_FIRST else c % 2) for c in range(8)]
F32, BF16 = jnp.float32, jnp.bfloat16
SPARE = 128
NT = (((1,), (1,)), ((), ()))
TN = (((0,), (0,)), ((), ()))


def sigmoid(x):
    return 0.5 * jnp.tanh(0.5 * x) + 0.5


def layer_norm(x, gain, bias, axis):
    mean = jnp.mean(x, axis=axis, keepdims=True)
    centred = x - mean
    var = jnp.mean(centred * centred, axis=axis, keepdims=True)
    return centred * lax.rsqrt(var + EPS) * gain + bias


def column(row):
    return jnp.broadcast_to(row, (8, 128)).T[:, :1]


def full(*shape):
    return pl.BlockSpec(shape, lambda i: (0,) * len(shape))


def rows_of(at, pair, zl, rows):
    return pl.ds((PAIR[pair] + STEP["zl"] * zl) * rows + at, 8, stride=B_STEP * rows)


def project_kernel(
    pair_hbm, mask_hbm, gain_hbm, bias_hbm, w_hbm, w_gate_hbm, out_ref, gate_ref,
    pair_ref, mask_ref, gain_ref, bias_ref, w_ref, w_gate_ref, wt_ref, normed_ref, wide_ref, sems,
):
    small = [
        pltpu.make_async_copy(src, dst, sems.at[6 + n])
        for n, (src, dst) in enumerate(
            (
                (w_hbm, w_ref),
                (gain_hbm, gain_ref),
                (bias_hbm, bias_ref),
                (mask_hbm, mask_ref),
                (w_gate_hbm, w_gate_ref),
            )
        )
    ]
    chunks = [
        pltpu.make_async_copy(pair_hbm.at[pl.ds(part * 8, 8)], pair_ref.at[pl.ds(part * 8, 8)], sems.at[part])
        for part in range(6)
    ]
    for copy in small + chunks:
        copy.start()
    lane = lax.broadcasted_iota(jnp.int32, (48, 384), 1)
    row = lax.broadcasted_iota(jnp.int32, (48, 384), 0)
    spread = (lane // 128 * 16 + lane % 16 == row).astype(F32).astype(BF16)
    own = lax.broadcasted_iota(jnp.int32, (8, 384), 1) // 16 % 8 == lax.broadcasted_iota(jnp.int32, (8, 384), 0)
    for copy in small:
        copy.wait()
    wt_ref[...] = w_ref[...].astype(F32).T.astype(BF16)
    keeps = jnp.dot(mask_ref[...].astype(F32).astype(BF16), spread, preferred_element_type=F32)
    gain, bias = column(gain_ref[...]), column(bias_ref[...])
    for copy in chunks[:2]:
        copy.wait()

    def norm(part):
        x = pair_ref[part * 8 : part * 8 + 8].reshape(8, 3, 16, 128).transpose(1, 0, 2, 3).reshape(384, 128)
        return layer_norm(x.T, gain, bias, 0).astype(BF16)

    for part in range(2):
        normed_ref[part] = norm(part)
    for copy in chunks[2:]:
        copy.wait()
    for part in range(6):
        normed = normed_ref[part] if part < 2 else norm(part)
        keep = jnp.sum(jnp.where(own, keeps[part * 8 : part * 8 + 8], 0.0), axis=0, keepdims=True)
        for side in range(2):
            gate = jnp.dot(wt_ref[side * 256 : side * 256 + 128, :], normed, preferred_element_type=F32)
            value = jnp.dot(wt_ref[side * 256 + 128 : side * 256 + 256, :], normed, preferred_element_type=F32)
            out = keep * sigmoid(gate) * value
            for kk_hi in range(3):
                at = side * 18 + part * 3 + kk_hi
                wide_ref[pl.ds(at, 128, stride=36), :] = out[:, kk_hi * 128 : kk_hi * 128 + 128]
        gate = sigmoid(lax.dot_general(normed, w_gate_ref[...], TN, preferred_element_type=F32))
        gate_ref[part * 8 : part * 8 + 8] = gate.reshape(3, 8, 16, 128).transpose(1, 0, 2, 3).reshape(8, 48, 128)
    out_ref[...] = wide_ref[:4608, :].astype(BF16)


def project(pair, mask, gain, bias, w_proj, w_gate):
    return pl.pallas_call(
        project_kernel,
        out_shape=(pltpu.VMEM((4608, 128), BF16), pltpu.VMEM((48, 48, 128), F32)),
        in_specs=[pl.BlockSpec(memory_space=pltpu.HBM)] * 6,
        out_specs=(pl.BlockSpec(memory_space=pltpu.VMEM), pl.BlockSpec(memory_space=pltpu.VMEM)),
        scratch_shapes=[
            pltpu.VMEM((48, 48, 128), F32),
            pltpu.VMEM((48, 48), jnp.int32),
            pltpu.VMEM((1, 128), F32),
            pltpu.VMEM((1, 128), F32),
            pltpu.VMEM((128, 512), BF16),
            pltpu.VMEM((128, 128), BF16),
            pltpu.VMEM((512, 128), BF16),
            pltpu.VMEM((6, 128, 384), BF16),
            pltpu.VMEM((4608 + SPARE, 128), F32),
            pltpu.SemaphoreType.DMA((11,)),
        ],
        compiler_params=pltpu.CompilerParams(vmem_limit_bytes=32 << 20),
        name="project",
    )(*(pltpu.with_memory_space_constraint(x, pltpu.HBM) for x in (pair, mask, gain, bias, w_proj, w_gate)))


def gather_left_kernel(recv_ref, swap_ref, out_ref, wide_ref, x_ref):
    wide_ref[:4608, :] = recv_ref[...].astype(F32)
    for s in range(18):
        for c in range(8):
            rows = [wide_ref[rows_of(s, c, zl, 36), :] for zl in range(2)]
            x_ref[s * 16 : s * 16 + 16, c * 128 : c * 128 + 128] = jnp.concatenate(rows).astype(BF16)
    for n in range(4):
        y = jnp.dot(x_ref[...], swap_ref[:, n * 256 : n * 256 + 256], preferred_element_type=F32).astype(BF16)
        for half in range(2):
            for s in range(18):
                at = (s // 3 * 8 + 2 * n + half) * 16
                lanes = slice(s % 3 * 128, s % 3 * 128 + 128)
                out_ref[at : at + 16, lanes] = y[s * 16 : s * 16 + 16, half * 128 : half * 128 + 128]


def gather_right_kernel(of_ref, recv_ref, swap_ref, out_ref, wide_ref, x_ref, rows_ref):
    wide_ref[:2304, :] = recv_ref[pl.ds(pl.multiple_of(of_ref[0] * 2304, 2304), 2304), :].astype(F32)
    for s in range(0, 18, 2):
        for c in range(8):
            rows = [wide_ref[rows_of(18 + s + k, c, 0, 36), :] for k in range(2)]
            x_ref[s * 8 : s * 8 + 16, c * 128 : c * 128 + 128] = jnp.concatenate(rows).astype(BF16)
    for n in range(4):
        y = jnp.dot(x_ref[...], swap_ref[:, n * 256 : n * 256 + 256], preferred_element_type=F32)
        for half in range(2):
            for s in range(18):
                at = (s // 3 * 8 + 2 * n + half) * 8
                rows_ref[s % 3, at : at + 8, :] = y[s * 8 : s * 8 + 8, half * 128 : half * 128 + 128]
    for kk_hi in range(3):
        for jj_hi in range(3):
            for b in range(8):
                at = (jj_hi * 8 + b) * 16
                rows = rows_ref[kk_hi, pl.ds(jj_hi * 128 + b, 16, stride=8), :]
                out_ref[at : at + 16, kk_hi * 128 : kk_hi * 128 + 128] = rows.astype(BF16)


def gather_left(recv, swap):
    return pl.pallas_call(
        gather_left_kernel,
        out_shape=jax.ShapeDtypeStruct((768, 384), BF16),
        scratch_shapes=[pltpu.VMEM((4608 + SPARE, 128), F32), pltpu.VMEM((288, 1024), BF16)],
        compiler_params=pltpu.CompilerParams(vmem_limit_bytes=32 << 20),
        name="gather_left",
    )(recv, swap)


def gather_right(of, recv, swap):
    vmem = pl.BlockSpec(memory_space=pltpu.VMEM)
    return pl.pallas_call(
        gather_right_kernel,
        out_shape=jax.ShapeDtypeStruct((384, 384), BF16),
        in_specs=[pl.BlockSpec(memory_space=pltpu.SMEM), vmem, vmem],
        out_specs=vmem,
        scratch_shapes=[
            pltpu.VMEM((2304 + SPARE, 128), F32),
            pltpu.VMEM((144, 1024), BF16),
            pltpu.VMEM((3, 384 + SPARE, 128), F32),
        ],
        compiler_params=pltpu.CompilerParams(vmem_limit_bytes=32 << 20),
        name="gather_right",
    )(of, recv, swap)


def contract_own_kernel(left_ref, right_ref, out_ref):
    for i in range(6):
        rows = slice(i * 128, i * 128 + 128)
        out_ref[rows, :] = lax.dot_general(left_ref[rows, :], right_ref[...], NT, preferred_element_type=F32)


def contract_own(left, right):
    return pl.pallas_call(
        contract_own_kernel,
        out_shape=jax.ShapeDtypeStruct((768, 384), F32),
        compiler_params=pltpu.CompilerParams(vmem_limit_bytes=32 << 20),
        cost_estimate=pl.CostEstimate(flops=2 * 768 * 384 * 384, bytes_accessed=2_000_000, transcendentals=0),
        name="contract_own",
    )(left, right)


def contract_kernel(own_ref, left_ref, right_ref, swap_ref, out_ref, x_ref, wide_ref):
    for i in range(6):
        rows = slice(i * 128, i * 128 + 128)
        mixed = lax.dot_general(left_ref[rows, :], right_ref[...], NT, preferred_element_type=F32)
        mixed = (own_ref[rows, :] + mixed).astype(BF16)
        for j in range(3):
            for a in range(8):
                at = (i * 3 + j) * 16
                x_ref[at : at + 16, a * 128 : a * 128 + 128] = mixed[a * 16 : a * 16 + 16, j * 128 : j * 128 + 128]
    for n in range(4):
        y = jnp.dot(x_ref[...], swap_ref[:, n * 256 : n * 256 + 256], preferred_element_type=F32)
        for half in range(2):
            for s in range(18):
                for zl in range(2):
                    at = s * 16 + zl * 8
                    wide_ref[rows_of(s, 2 * n + half, zl, 18), :] = y[at : at + 8, half * 128 : half * 128 + 128]
    out_ref[...] = wide_ref[:2304, :].astype(BF16)


def contract(own, left, right, swap):
    return pl.pallas_call(
        contract_kernel,
        out_shape=jax.ShapeDtypeStruct((2304, 128), BF16),
        scratch_shapes=[pltpu.VMEM((288, 1024), BF16), pltpu.VMEM((2304 + SPARE, 128), F32)],
        compiler_params=pltpu.CompilerParams(vmem_limit_bytes=32 << 20),
        name="contract",
    )(own, left, right, swap)


def finish_kernel(mixed_ref, gate_ref, gain_ref, bias_ref, w_ref, out_hbm, wide_ref, out_ref, sems):
    wide_ref[:2304, :] = mixed_ref[...].astype(F32)
    gain, bias = column(gain_ref[...]), column(bias_ref[...])
    copies = []
    for part in range(6):
        for jj_hi in range(3):
            mixed = wide_ref[pl.ds(part * 3 + jj_hi, 128, stride=18), :]
            normed = layer_norm(mixed, gain, bias, 0).astype(BF16)
            projected = lax.dot_general(normed, w_ref[...], TN, preferred_element_type=F32).reshape(8, 16, 128)
            rows, cols = slice(part * 8, part * 8 + 8), slice(jj_hi * 16, jj_hi * 16 + 16)
            out_ref[rows, cols, :] = gate_ref[rows, cols, :] * projected
        rows = pl.ds(part * 8, 8)
        copies.append(pltpu.make_async_copy(out_ref.at[rows], out_hbm.at[rows], sems.at[part]))
        copies[-1].start()
    for copy in copies:
        copy.wait()


def finish(mixed, gate, gain, bias, w_out):
    return pl.pallas_call(
        finish_kernel,
        out_shape=jax.ShapeDtypeStruct((48, 48, 128), F32),
        in_specs=[pl.BlockSpec(memory_space=pltpu.VMEM)] * 5,
        out_specs=pl.BlockSpec(memory_space=pltpu.HBM),
        scratch_shapes=[
            pltpu.VMEM((2304 + SPARE, 128), F32),
            pltpu.VMEM((48, 48, 128), F32),
            pltpu.SemaphoreType.DMA((6,)),
        ],
        compiler_params=pltpu.CompilerParams(vmem_limit_bytes=32 << 20),
        name="finish",
    )(mixed, gate, gain, bias, w_out)


def exchange(messages):
    rows = messages.shape[0] // 128
    tiles = messages.reshape(128, 9, rows // 9, 128)
    return lax.all_to_all(tiles, GROUP, 0, 0, tiled=True).reshape(128 * rows, 128)


def per_device(pair, pair_mask, ln_gain, ln_bias, w_proj, w_gate, out_gain, out_bias, w_out):
    hold = lax.optimization_barrier
    sent, gate = project(pair, pair_mask, ln_gain.reshape(1, 128), ln_bias.reshape(1, 128), w_proj, w_gate)
    core = lax.axis_index("core").astype(jnp.int32).reshape(1)
    sent, gate, core, other = hold((sent, gate, core, 1 - core))
    recv, gate, w_out, out_gain, out_bias = hold((exchange(sent), gate, w_out, out_gain, out_bias))
    place = np.arange(1024)
    swap = jnp.asarray(place[None, :] == (place // 16 % 8 * 128 + place // 128 * 16 + place % 16)[:, None], BF16)
    swap_cores = lambda v: lax.ppermute(v, "core", [(0, 1), (1, 0)])
    left, right2 = hold((gather_left(recv, swap), gather_right(other, recv, swap)))
    left2, right2 = swap_cores(left), swap_cores(right2)
    right = gather_right(core, recv, swap)
    own = contract_own(left, right)
    sent = contract(own, left2, right2, swap)
    sent, gate, w_out, out_gain, out_bias = hold((sent, gate, w_out, out_gain, out_bias))
    mixed, gate, w_out, out_gain, out_bias = hold((exchange(sent), gate, w_out, out_gain, out_bias))
    return finish(mixed, gate, out_gain.reshape(1, 128), out_bias.reshape(1, 128), w_out)


def solution(mesh):
    fine = Mesh(mesh.devices.reshape(2, 4, 2, 2, 4, 2), ROW + COL)
    return jax.shard_map(
        per_device,
        mesh=fine,
        in_specs=(P(ROW, COL, None), P(ROW, COL), P(), P(), P(), P(), P(), P(), P()),
        out_specs=P(ROW, COL, None),
        check_vma=False,
    )
```

```python
import math

import jax
import jax.numpy as jnp
import numpy as np
from jax import lax
from jax.experimental import pallas as pl
from jax.experimental.pallas import tpu as pltpu
from jax.sharding import Mesh, PartitionSpec as P

EPS = 1e-05
ROW = ("xh", "zh", "zl")
COL = ("xl", "y", "core")
GROUP = ("zl", "y", "zh", "xh", "xl")
SIZES = dict(zh=4, zl=2, xl=2, y=4, xh=2)
STEP = {axis: math.prod(SIZES[later] for later in GROUP[n + 1 :]) for n, axis in enumerate(GROUP)}
XH_FIRST = GROUP.index("xh") < GROUP.index("zh")
B_STEP = STEP["zh" if XH_FIRST else "xh"]
PAIR = [STEP["y"] * (c % 4 if XH_FIRST else c // 2) + STEP["xl"] * (c // 4 if XH_FIRST else c % 2) for c in range(8)]
F32, BF16 = jnp.float32, jnp.bfloat16
SPARE = 128
NT = (((1,), (1,)), ((), ()))
TN = (((0,), (0,)), ((), ()))


def sigmoid(x):
    return 0.5 * jnp.tanh(0.5 * x) + 0.5


def layer_norm(x, gain, bias, axis):
    mean = jnp.mean(x, axis=axis, keepdims=True)
    centred = x - mean
    var = jnp.mean(centred * centred, axis=axis, keepdims=True)
    return centred * lax.rsqrt(var + EPS) * gain + bias


def column(row):
    return jnp.broadcast_to(row, (8, 128)).T[:, :1]


def full(*shape):
    return pl.BlockSpec(shape, lambda i: (0,) * len(shape))


def rows_of(at, pair, zl, rows):
    return pl.ds((PAIR[pair] + STEP["zl"] * zl) * rows + at, 8, stride=B_STEP * rows)


def project_kernel(
    pair_hbm, mask_hbm, gain_hbm, bias_hbm, w_hbm, w_gate_hbm, out_ref, gate_ref,
    pair_ref, mask_ref, gain_ref, bias_ref, w_ref, w_gate_ref, wt_ref, normed_ref, wide_ref, sems,
):
    small = [
        pltpu.make_async_copy(src, dst, sems.at[6 + n])
        for n, (src, dst) in enumerate(
            (
                (w_hbm, w_ref),
                (gain_hbm, gain_ref),
                (bias_hbm, bias_ref),
                (mask_hbm, mask_ref),
                (w_gate_hbm, w_gate_ref),
            )
        )
    ]
    chunks = [
        pltpu.make_async_copy(pair_hbm.at[pl.ds(part * 8, 8)], pair_ref.at[pl.ds(part * 8, 8)], sems.at[part])
        for part in range(6)
    ]
    for copy in small + chunks:
        copy.start()
    lane = lax.broadcasted_iota(jnp.int32, (48, 384), 1)
    row = lax.broadcasted_iota(jnp.int32, (48, 384), 0)
    spread = (lane // 128 * 16 + lane % 16 == row).astype(F32).astype(BF16)
    own = lax.broadcasted_iota(jnp.int32, (8, 384), 1) // 16 % 8 == lax.broadcasted_iota(jnp.int32, (8, 384), 0)
    for copy in small:
        copy.wait()
    wt_ref[...] = w_ref[...].astype(F32).T.astype(BF16)
    keeps = jnp.dot(mask_ref[...].astype(F32).astype(BF16), spread, preferred_element_type=F32)
    gain, bias = column(gain_ref[...]), column(bias_ref[...])
    for copy in chunks[:2]:
        copy.wait()

    def norm(part):
        x = pair_ref[part * 8 : part * 8 + 8].reshape(8, 3, 16, 128).transpose(1, 0, 2, 3).reshape(384, 128)
        return layer_norm(x.T, gain, bias, 0).astype(BF16)

    for part in range(2):
        normed_ref[part] = norm(part)
    for copy in chunks[2:]:
        copy.wait()
    for part in range(6):
        normed = normed_ref[part] if part < 2 else norm(part)
        keep = jnp.sum(jnp.where(own, keeps[part * 8 : part * 8 + 8], 0.0), axis=0, keepdims=True)
        for side in range(2):
            gate = jnp.dot(wt_ref[side * 256 : side * 256 + 128, :], normed, preferred_element_type=F32)
            value = jnp.dot(wt_ref[side * 256 + 128 : side * 256 + 256, :], normed, preferred_element_type=F32)
            out = keep * sigmoid(gate) * value
            for kk_hi in range(3):
                at = side * 18 + part * 3 + kk_hi
                wide_ref[pl.ds(at, 128, stride=36), :] = out[:, kk_hi * 128 : kk_hi * 128 + 128]
        gate = sigmoid(lax.dot_general(normed, w_gate_ref[...], TN, preferred_element_type=F32))
        gate_ref[part * 8 : part * 8 + 8] = gate.reshape(3, 8, 16, 128).transpose(1, 0, 2, 3).reshape(8, 48, 128)
    out_ref[...] = wide_ref[:4608, :].astype(BF16)


def project(pair, mask, gain, bias, w_proj, w_gate):
    return pl.pallas_call(
        project_kernel,
        out_shape=(pltpu.VMEM((4608, 128), BF16), pltpu.VMEM((48, 48, 128), F32)),
        in_specs=[pl.BlockSpec(memory_space=pltpu.HBM)] * 6,
        out_specs=(pl.BlockSpec(memory_space=pltpu.VMEM), pl.BlockSpec(memory_space=pltpu.VMEM)),
        scratch_shapes=[
            pltpu.VMEM((48, 48, 128), F32),
            pltpu.VMEM((48, 48), jnp.int32),
            pltpu.VMEM((1, 128), F32),
            pltpu.VMEM((1, 128), F32),
            pltpu.VMEM((128, 512), BF16),
            pltpu.VMEM((128, 128), BF16),
            pltpu.VMEM((512, 128), BF16),
            pltpu.VMEM((6, 128, 384), BF16),
            pltpu.VMEM((4608 + SPARE, 128), F32),
            pltpu.SemaphoreType.DMA((11,)),
        ],
        compiler_params=pltpu.CompilerParams(vmem_limit_bytes=32 << 20),
        name="project",
    )(*(pltpu.with_memory_space_constraint(x, pltpu.HBM) for x in (pair, mask, gain, bias, w_proj, w_gate)))


def gather_left_kernel(recv_ref, swap_ref, out_ref, wide_ref, x_ref):
    wide_ref[:4608, :] = recv_ref[...].astype(F32)
    for s in range(18):
        for c in range(8):
            rows = [wide_ref[rows_of(s, c, zl, 36), :] for zl in range(2)]
            x_ref[s * 16 : s * 16 + 16, c * 128 : c * 128 + 128] = jnp.concatenate(rows).astype(BF16)
    for n in range(4):
        y = jnp.dot(x_ref[...], swap_ref[:, n * 256 : n * 256 + 256], preferred_element_type=F32).astype(BF16)
        for half in range(2):
            for s in range(18):
                at = (s // 3 * 8 + 2 * n + half) * 16
                lanes = slice(s % 3 * 128, s % 3 * 128 + 128)
                out_ref[at : at + 16, lanes] = y[s * 16 : s * 16 + 16, half * 128 : half * 128 + 128]


def gather_right_kernel(of_ref, recv_ref, swap_ref, out_ref, wide_ref, x_ref, rows_ref):
    wide_ref[:2304, :] = recv_ref[pl.ds(pl.multiple_of(of_ref[0] * 2304, 2304), 2304), :].astype(F32)
    for s in range(0, 18, 2):
        for c in range(8):
            rows = [wide_ref[rows_of(18 + s + k, c, 0, 36), :] for k in range(2)]
            x_ref[s * 8 : s * 8 + 16, c * 128 : c * 128 + 128] = jnp.concatenate(rows).astype(BF16)
    for n in range(4):
        y = jnp.dot(x_ref[...], swap_ref[:, n * 256 : n * 256 + 256], preferred_element_type=F32)
        for half in range(2):
            for s in range(18):
                at = (s // 3 * 8 + 2 * n + half) * 8
                rows_ref[s % 3, at : at + 8, :] = y[s * 8 : s * 8 + 8, half * 128 : half * 128 + 128]
    for kk_hi in range(3):
        for jj_hi in range(3):
            for b in range(8):
                at = (jj_hi * 8 + b) * 16
                rows = rows_ref[kk_hi, pl.ds(jj_hi * 128 + b, 16, stride=8), :]
                out_ref[at : at + 16, kk_hi * 128 : kk_hi * 128 + 128] = rows.astype(BF16)


def gather_left(recv, swap):
    return pl.pallas_call(
        gather_left_kernel,
        out_shape=jax.ShapeDtypeStruct((768, 384), BF16),
        scratch_shapes=[pltpu.VMEM((4608 + SPARE, 128), F32), pltpu.VMEM((288, 1024), BF16)],
        compiler_params=pltpu.CompilerParams(vmem_limit_bytes=32 << 20),
        name="gather_left",
    )(recv, swap)


def gather_right(of, recv, swap):
    vmem = pl.BlockSpec(memory_space=pltpu.VMEM)
    return pl.pallas_call(
        gather_right_kernel,
        out_shape=jax.ShapeDtypeStruct((384, 384), BF16),
        in_specs=[pl.BlockSpec(memory_space=pltpu.SMEM), vmem, vmem],
        out_specs=vmem,
        scratch_shapes=[
            pltpu.VMEM((2304 + SPARE, 128), F32),
            pltpu.VMEM((144, 1024), BF16),
            pltpu.VMEM((3, 384 + SPARE, 128), F32),
        ],
        compiler_params=pltpu.CompilerParams(vmem_limit_bytes=32 << 20),
        name="gather_right",
    )(of, recv, swap)


def contract_own_kernel(left_ref, right_ref, out_ref):
    for i in range(6):
        rows = slice(i * 128, i * 128 + 128)
        out_ref[rows, :] = lax.dot_general(left_ref[rows, :], right_ref[...], NT, preferred_element_type=F32)


def contract_own(left, right):
    return pl.pallas_call(
        contract_own_kernel,
        out_shape=jax.ShapeDtypeStruct((768, 384), F32),
        compiler_params=pltpu.CompilerParams(vmem_limit_bytes=32 << 20),
        cost_estimate=pl.CostEstimate(flops=2 * 768 * 384 * 384, bytes_accessed=2_000_000, transcendentals=0),
        name="contract_own",
    )(left, right)


def contract_kernel(own_ref, left_ref, right_ref, swap_ref, out_ref, x_ref, wide_ref):
    for i in range(6):
        rows = slice(i * 128, i * 128 + 128)
        mixed = lax.dot_general(left_ref[rows, :], right_ref[...], NT, preferred_element_type=F32)
        mixed = (own_ref[rows, :] + mixed).astype(BF16)
        for j in range(3):
            for a in range(8):
                at = (i * 3 + j) * 16
                x_ref[at : at + 16, a * 128 : a * 128 + 128] = mixed[a * 16 : a * 16 + 16, j * 128 : j * 128 + 128]
    for n in range(4):
        y = jnp.dot(x_ref[...], swap_ref[:, n * 256 : n * 256 + 256], preferred_element_type=F32)
        for half in range(2):
            for s in range(18):
                for zl in range(2):
                    at = s * 16 + zl * 8
                    wide_ref[rows_of(s, 2 * n + half, zl, 18), :] = y[at : at + 8, half * 128 : half * 128 + 128]
    out_ref[...] = wide_ref[:2304, :].astype(BF16)


def contract(own, left, right, swap):
    return pl.pallas_call(
        contract_kernel,
        out_shape=jax.ShapeDtypeStruct((2304, 128), BF16),
        scratch_shapes=[pltpu.VMEM((288, 1024), BF16), pltpu.VMEM((2304 + SPARE, 128), F32)],
        compiler_params=pltpu.CompilerParams(vmem_limit_bytes=32 << 20),
        name="contract",
    )(own, left, right, swap)


def finish_kernel(mixed_ref, gate_ref, gain_ref, bias_ref, w_ref, out_hbm, wide_ref, out_ref, sems):
    wide_ref[:2304, :] = mixed_ref[...].astype(F32)
    gain, bias = column(gain_ref[...]), column(bias_ref[...])
    copies = []
    for part in range(6):
        for jj_hi in range(3):
            mixed = wide_ref[pl.ds(part * 3 + jj_hi, 128, stride=18), :]
            normed = layer_norm(mixed, gain, bias, 0).astype(BF16)
            projected = lax.dot_general(normed, w_ref[...], TN, preferred_element_type=F32).reshape(8, 16, 128)
            rows, cols = slice(part * 8, part * 8 + 8), slice(jj_hi * 16, jj_hi * 16 + 16)
            out_ref[rows, cols, :] = gate_ref[rows, cols, :] * projected
        rows = pl.ds(part * 8, 8)
        copies.append(pltpu.make_async_copy(out_ref.at[rows], out_hbm.at[rows], sems.at[part]))
        copies[-1].start()
    for copy in copies:
        copy.wait()


def finish(mixed, gate, gain, bias, w_out):
    return pl.pallas_call(
        finish_kernel,
        out_shape=jax.ShapeDtypeStruct((48, 48, 128), F32),
        in_specs=[pl.BlockSpec(memory_space=pltpu.VMEM)] * 5,
        out_specs=pl.BlockSpec(memory_space=pltpu.HBM),
        scratch_shapes=[
            pltpu.VMEM((2304 + SPARE, 128), F32),
            pltpu.VMEM((48, 48, 128), F32),
            pltpu.SemaphoreType.DMA((6,)),
        ],
        compiler_params=pltpu.CompilerParams(vmem_limit_bytes=32 << 20),
        name="finish",
    )(mixed, gate, gain, bias, w_out)


def exchange(messages):
    rows = messages.shape[0] // 128
    tiles = messages.reshape(128, 9, rows // 9, 128)
    return lax.all_to_all(tiles, GROUP, 0, 0, tiled=True).reshape(128 * rows, 128)


def per_device(pair, pair_mask, ln_gain, ln_bias, w_proj, w_gate, out_gain, out_bias, w_out):
    hold = lax.optimization_barrier
    sent, gate = project(pair, pair_mask, ln_gain.reshape(1, 128), ln_bias.reshape(1, 128), w_proj, w_gate)
    core = lax.axis_index("core").astype(jnp.int32).reshape(1)
    sent, gate, core, other = hold((sent, gate, core, 1 - core))
    recv, gate, w_out, out_gain, out_bias = hold((exchange(sent), gate, w_out, out_gain, out_bias))
    place = np.arange(1024)
    swap = jnp.asarray(place[None, :] == (place // 16 % 8 * 128 + place // 128 * 16 + place % 16)[:, None], BF16)
    swap_cores = lambda v: lax.ppermute(v, "core", [(0, 1), (1, 0)])
    left = gather_left(recv, swap)
    left2 = swap_cores(left)
    right2 = swap_cores(gather_right(other, recv, swap))
    right = gather_right(core, recv, swap)
    own = contract_own(left, right)
    sent = contract(own, left2, right2, swap)
    sent, gate, w_out, out_gain, out_bias = hold((sent, gate, w_out, out_gain, out_bias))
    mixed, gate, w_out, out_gain, out_bias = hold((exchange(sent), gate, w_out, out_gain, out_bias))
    return finish(mixed, gate, out_gain.reshape(1, 128), out_bias.reshape(1, 128), w_out)


def solution(mesh):
    fine = Mesh(mesh.devices.reshape(2, 4, 2, 2, 4, 2), ROW + COL)
    return jax.shard_map(
        per_device,
        mesh=fine,
        in_specs=(P(ROW, COL, None), P(ROW, COL), P(), P(), P(), P(), P(), P(), P()),
        out_specs=P(ROW, COL, None),
        check_vma=False,
    )
```
